32 devices in a mesh: dp: 2 (over x), fsdp: 16 (over z, y, core).
Axes of the slice: x: 2, y: 2, z: 4, core: 2. Of those that a mesh axis runs over, the one named last changes fastest.
Arguments:
- tokens: bfloat16 [4096, 3584], P(('dp', 'fsdp')), may hold values from -6 to 6
- out_grad: bfloat16 [4096, 14336], P(('dp', 'fsdp')), may hold values from -6 to 6
- block_values: bfloat16 [80, 128, 128], P('fsdp'), may hold values from -0.625 to 0.625
- active_blocks: int32 [80, 2], P('fsdp'), may hold values from 0 to 111, as said below
- drop_slots: int32 [16], P('fsdp'), may hold values from 0 to 4, as said below
- cand_blocks: int32 [16, 2], replicated, may hold values from 0 to 111, as said below
- group_counts: int32 [2], P('dp'), may hold values from 1024 to 2048
Outputs:
- cand_grad: float32 [16, 128, 128], P('fsdp')
- cand_score: float32 [16], P('fsdp')
The draws below stay inside these ranges and needn't reach their ends.
Inputs may be any that keep to these rules, and one draw needn't show every extreme that they name: `active_blocks`: pairs of block row (below D / 128) and block column (below 14336 / 128); all pairs distinct. `drop_slots`: the 1 entries of each device are distinct local slots. `cand_blocks`: pairs of block row and block column, distinct, none of them a stored block.
All inputs are finite; a program needn't handle non-finite values.
Results may differ from the reference program's by a relative error of at most 0.007.
Values may be sent and summed in bfloat16 or wider, within the bound.
A program may use at most 128 MiB of HBM per device.

```python
import math
import jax
import jax.numpy as jnp
from jax import lax

D = 3584
FF = 14336
BLK = 128
TOK_DEV = 128
K_DEV = 5
DROP_DEV = 1
GROUP_TOK = 2048
TOKENS = 4096
K = 80
DROPS = 16
CANDS = 16
N_DP = 2
N_FSDP = 16


def block_order(key):
    return jax.random.permutation(key, D // BLK * (FF // BLK)).astype(jnp.int32)


def draw_active_blocks(key, part):
    shared = block_order(key)[:K]
    return jnp.stack([shared // (FF // BLK), shared % (FF // BLK)], axis=1).astype(jnp.int32)


def draw_cand_blocks(key, part):
    shared = block_order(key)[K:K + CANDS]
    return jnp.stack([shared // (FF // BLK), shared % (FF // BLK)], axis=1).astype(jnp.int32)


def draw_drop_slots(key, part):
    key = jax.random.fold_in(key, 3)
    subkeys = jax.random.split(key, K // K_DEV)
    picked = jax.vmap(lambda single: jax.random.permutation(single, K_DEV)[:DROP_DEV])(subkeys)
    return picked.reshape(-1).astype(jnp.int32)


def block_scale(stream_key, shape, shards, low, top_value):
    def one(axis_at, parts):
        heights = jax.random.uniform(jax.random.fold_in(jax.random.fold_in(stream_key, 6), axis_at), (parts,), jnp.float32, low / len(shards), top_value / len(shards))
        return jnp.repeat(jnp.exp(heights), shape[axis_at] // parts).reshape((-1,) + (1,) * (len(shape) - axis_at - 1))

    gain = one(*shards[0])
    for cut in shards[1:]:
        gain = gain * one(*cut)
    return gain


def noise(stream_key, dims, scale, bound, pieces=(), kind=jnp.bfloat16):
    entries = jax.random.normal(stream_key, dims, jnp.float32) * scale
    if len(pieces) > 0:
        entries = block_scale(stream_key, dims, pieces, -0.22, 0.18) * entries
    return jnp.clip(entries, min=-bound, max=bound).astype(kind)


def setup_inputs(seed: int = 0) -> dict:
    keys = jax.random.split(jax.random.key(seed), 8)
    tokens = noise(keys[0], (TOKENS, D), 1.0, 6.0, ((0, 32),))
    out_grad = noise(keys[1], (TOKENS, FF), 1.0, 6.0, ((0, 32),))
    block_values = noise(keys[2], (K, BLK, BLK), (K * BLK * BLK // FF) ** -0.5, 0.625, ((0, 16),))
    active_blocks = draw_active_blocks(jax.random.fold_in(keys[7], 71), 0)
    drop_slots = draw_drop_slots(jax.random.fold_in(keys[7], 71), 0)
    cand_blocks = draw_cand_blocks(jax.random.fold_in(keys[7], 71), 0)
    group_counts = jax.random.randint(keys[6], (N_DP,), GROUP_TOK // 2, GROUP_TOK + 1).astype(jnp.int32)
    return dict(tokens=tokens, out_grad=out_grad, block_values=block_values, active_blocks=active_blocks, drop_slots=drop_slots, cand_blocks=cand_blocks, group_counts=group_counts)


def gelu_slope(value_in):
    normal_cdf = 0.5 * (1.0 + jax.scipy.special.erf(value_in * 0.7071067811865476))
    density = jnp.exp(-0.5 * value_in * value_in) * 0.3989422804014327
    return normal_cdf + value_in * density

def reference(tokens, out_grad, block_values, active_blocks, drop_slots, cand_blocks, group_counts):
    row_blocks = D // BLK
    col_blocks = FF // BLK
    owners = jnp.arange(DROPS, dtype=jnp.int32) // DROP_DEV
    kept_flag = jnp.ones((K,), jnp.float32).at[owners * K_DEV + drop_slots].set(0.0)
    weights = block_values.astype(jnp.float32) * kept_flag[:, None, None]
    block_rows = active_blocks[:, 0]
    block_cols = active_blocks[:, 1]
    cand_rows = cand_blocks[:, 0]
    cand_cols = cand_blocks[:, 1]
    devices_all = N_DP * N_FSDP
    tok_split = tokens.reshape(devices_all, TOK_DEV, row_blocks, BLK)
    grad_split = out_grad.reshape(devices_all, TOK_DEV, FF)

    def advance(summed, sliced):
        device_id, tok_block, grad_block = sliced
        picked = tok_block[:, block_rows, :].astype(jnp.float32)
        product = jnp.einsum('tkb,kbc->tkc', picked, weights)
        preact = jnp.zeros((TOK_DEV, col_blocks, BLK), jnp.float32).at[:, block_cols, :].add(product)
        preact = preact.reshape(TOK_DEV, FF)
        group_id = device_id // N_FSDP
        position = device_id % N_FSDP * TOK_DEV + jnp.arange(TOK_DEV, dtype=jnp.int32)
        usable = (position < group_counts[group_id]).astype(jnp.float32)
        pre_grad = (grad_block.astype(jnp.float32) * gelu_slope(preact) * usable[:, None]).astype(jnp.bfloat16)
        cand_x = tok_block[:, cand_rows, :].astype(jnp.float32)
        cand_dy = pre_grad.reshape(TOK_DEV, col_blocks, BLK)[:, cand_cols, :].astype(jnp.float32)
        return (summed + jnp.einsum('tcb,tce->cbe', cand_x, cand_dy), None)
    summed, _ = lax.scan(advance, jnp.zeros((CANDS, BLK, BLK), jnp.float32), (jnp.arange(devices_all, dtype=jnp.int32), tok_split, grad_split))
    cand_grad = summed * (1.0 / math.sqrt(TOKENS))
    cand_score = jnp.sqrt(lax.optimization_barrier(jnp.mean(cand_grad * cand_grad, axis=(1, 2))) + 1e-06)
    return (cand_grad, cand_score)
```

```python
import functools
import jax
import jax.numpy as jnp
from jax import lax
from jax.experimental import pallas as pl
from jax.experimental.pallas import tpu as pltpu
from jax.sharding import PartitionSpec as P

MESH = pl.DeviceIdType.MESH


def gelu_slope(value_in):
    normal_cdf = 0.5 * (1.0 + lax.erf(value_in * 0.7071067811865476))
    density = jnp.exp(-0.5 * value_in * value_in) * 0.3989422804014327
    return normal_cdf + value_in * density


def kernel(
    dims,
    tok_hbm, og_hbm, bv_hbm, active, drops, cands, counts,
    grad_out, score_out,
    tok, og, bv, gath, meta_v, meta_s, xt, prod, acc,
    send_a, recv_a, own_a, send_c, recv_c, own_c, send_d, recv_d, share_b,
    load_sem, meta_send, meta_recv, meta_load, chunk_send, chunk_recv,
    a_send, a_recv, c_send, c_recv, d_send, d_recv, b_send, b_recv,
):
    n_dp, n_f, outer, inner = dims
    blk = bv.shape[1]
    stored = bv.shape[0]
    kept = stored - 1
    n_cand = acc.shape[0]
    dp = lax.axis_index("dp")
    me = lax.axis_index("fsdp")
    core = me % 2
    my_b = (me // 2) % inner
    my_a = me // (2 * inner)
    sibling = me + 1 - 2 * core

    def index(a, b, c):
        return (a * inner + b) * 2 + c

    load_bv = pltpu.make_async_copy(bv_hbm, bv, load_sem.at[0])
    load_bv.start()

    def load_columns(hbm, held, sem):
        @pl.loop(0, held.shape[0])
        def _(at):
            column = pl.multiple_of(at * blk, blk)
            pltpu.make_async_copy(hbm.at[:, pl.ds(column, blk)], held.at[at], sem).start()

    def wait_columns(held, sem):
        pltpu.make_async_copy(held, held, sem).wait()

    barrier = pltpu.get_barrier_semaphore()

    @pl.loop(1, n_f)
    def _(step):
        pl.semaphore_signal(
            barrier, inc=1, device_id={"fsdp": (me + step) % n_f}, device_id_type=MESH
        )

    @pl.loop(1, n_dp)
    def _(step):
        pl.semaphore_signal(
            barrier, inc=1, device_id={"dp": (dp + step) % n_dp}, device_id_type=MESH
        )

    load_columns(tok_hbm, tok, load_sem.at[1])
    drop = drops[0]
    lane = lax.broadcasted_iota(jnp.int32, (1, 128), 1)
    places = jnp.zeros((1, 128), jnp.int32)
    load_bv.wait()
    for slot in range(kept):
        at = slot + jnp.where(drop <= slot, 1, 0)
        gath[me, slot * blk:(slot + 1) * blk, :] = bv[at]
        places = jnp.where(lane == 2 * slot, active[at, 0], places)
        places = jnp.where(lane == 2 * slot + 1, active[at, 1], places)
    meta_v[me] = places

    pl.semaphore_wait(barrier, n_f - 1 + n_dp - 1)

    def chunk_copy(source, way, target):
        return pltpu.make_async_remote_copy(
            src_ref=gath.at[source],
            dst_ref=gath.at[source],
            send_sem=chunk_send.at[way, source],
            recv_sem=chunk_recv.at[source],
            device_id={"fsdp": target},
            device_id_type=MESH,
        )

    def meta_copy(step):
        target = (me + step) % n_f
        return pltpu.make_async_remote_copy(
            src_ref=meta_v.at[me],
            dst_ref=meta_v.at[me],
            send_sem=meta_send.at[step],
            recv_sem=meta_recv.at[me],
            device_id={"fsdp": target},
            device_id_type=MESH,
        )

    def meta_arrival(source):
        return pltpu.make_async_remote_copy(
            src_ref=meta_v.at[source],
            dst_ref=meta_v.at[source],
            send_sem=meta_send.at[0],
            recv_sem=meta_recv.at[source],
            device_id={"fsdp": sibling},
            device_id_type=MESH,
        )

    def forwards(a, b, act):
        source = index(a, b, core)

        @pl.when((b == my_b) & (a >= my_a) & (my_a > 0))
        def _():
            act(chunk_copy(source, 0, index(my_a - 1, my_b, core)))

        @pl.when((b == my_b) & (a <= my_a) & (my_a < outer - 1))
        def _():
            act(chunk_copy(source, 1, index(my_a + 1, my_b, core)))

        @pl.when((b >= my_b) & (my_b > 0))
        def _():
            act(chunk_copy(source, 2, index(my_a, my_b - 1, core)))

        @pl.when((b <= my_b) & (my_b < inner - 1))
        def _():
            act(chunk_copy(source, 3, index(my_a, my_b + 1, core)))

        act(chunk_copy(source, 4, sibling))

    def around(step, mine):
        return mine + (1 - 2 * (step % 2)) * ((step + 1) // 2)

    forwards(my_a, my_b, lambda copy: copy.start())

    @pl.loop(1, n_f)
    def _(step):
        meta_copy(step).start()

    load_columns(og_hbm, og, load_sem.at[2])
    wait_columns(tok, load_sem.at[1])

    @pl.loop(0, n_cand)
    def _(c):
        xt[c] = tok[cands[c, 0]].T
        acc[c] = jnp.zeros((blk, blk), jnp.float32)

    @pl.loop(1, n_f)
    def _(step):
        meta_arrival((me + step) % n_f).wait_recv()

    to_scalars = pltpu.make_async_copy(meta_v, meta_s, meta_load)
    to_scalars.start()
    to_scalars.wait()

    def process(source):
        for slot in range(kept):
            prod[slot] = jnp.dot(
                tok[meta_s[source, 0, 2 * slot]],
                gath[source, slot * blk:(slot + 1) * blk, :],
                preferred_element_type=jnp.float32,
            )
        columns = [meta_s[source, 0, 2 * slot + 1] for slot in range(kept)]

        @pl.loop(0, n_cand)
        def _(c):
            column = cands[c, 1]
            total = acc[c]
            for slot in range(kept):
                total = total + jnp.where(columns[slot] == column, 1.0, 0.0) * prod[slot]
            acc[c] = total

    @pl.loop(0, 2 * outer - 1)
    def _(i):
        a = around(i, my_a)

        @pl.loop(0, 2 * inner - 1)
        def _(j):
            b = around(j, my_b)

            @pl.when((a >= 0) & (a < outer) & (b >= 0) & (b < inner))
            def _():
                source = index(a, b, core)

                @pl.when(i + j > 0)
                def _():
                    chunk_copy(source, 4, sibling).wait_recv()
                    forwards(a, b, lambda copy: copy.start())

                process(source)
                other = index(a, b, 1 - core)
                chunk_copy(other, 4, sibling).wait_recv()
                process(other)

    wait_columns(og, load_sem.at[2])
    position = me * blk + lax.broadcasted_iota(jnp.int32, (blk, 1), 0)
    usable = jnp.where(position < counts[0], 1.0, 0.0)

    def term(c):
        slope = gelu_slope(acc[c])
        pre_grad = og[cands[c, 1]].astype(jnp.float32) * slope * usable
        return jnp.dot(xt[c], pre_grad.astype(jnp.bfloat16), preferred_element_type=jnp.float32)

    def a_copy(a, b):
        at = a * inner + b
        return pltpu.make_async_remote_copy(
            src_ref=send_a.at[at], dst_ref=recv_a.at[at],
            send_sem=a_send.at[at], recv_sem=a_recv.at[at],
            device_id={"fsdp": sibling}, device_id_type=MESH,
        )

    def c_copy(a, step):
        return pltpu.make_async_remote_copy(
            src_ref=send_c.at[step, a], dst_ref=recv_c.at[step, a],
            send_sem=c_send.at[step, a], recv_sem=c_recv.at[step, a],
            device_id={"fsdp": index(my_a, (my_b + step) % inner, core)}, device_id_type=MESH,
        )

    def d_copy(step):
        return pltpu.make_async_remote_copy(
            src_ref=send_d.at[step], dst_ref=recv_d.at[step],
            send_sem=d_send.at[step], recv_sem=d_recv.at[step],
            device_id={"fsdp": index((my_a + step) % outer, my_b, core)}, device_id_type=MESH,
        )

    def b_copy(step):
        return pltpu.make_async_remote_copy(
            src_ref=share_b.at[0], dst_ref=share_b.at[step],
            send_sem=b_send.at[step], recv_sem=b_recv.at[step],
            device_id={"dp": (dp + step) % n_dp}, device_id_type=MESH,
        )

    def every(act):
        @pl.loop(1, inner + 1)
        def _(step):
            b = (my_b + step) % inner

            @pl.loop(1, outer + 1)
            def _(hop):
                act(step, b, (my_a + hop) % outer)

    def for_sibling(step, b, a):
        send_a[a * inner + b] = term(index(a, b, 1 - core)).astype(jnp.bfloat16)
        a_copy(a, b).start()

    every(for_sibling)

    def for_mine(step, b, a):
        own_a[...] = term(index(a, b, core))
        a_copy(a, b).wait_recv()
        total = own_a[...] + recv_a[a * inner + b].astype(jnp.float32)

        @pl.when(step < inner)
        def _():
            send_c[step, a] = total.astype(jnp.bfloat16)
            c_copy(a, step).start()

        @pl.when(step == inner)
        def _():
            own_c[a] = total

    every(for_mine)

    @pl.loop(1, outer + 1)
    def _(hop):
        a = (my_a + hop) % outer
        total = own_c[a]
        for step in range(1, inner):
            c_copy(a, step).wait_recv()
            total = total + recv_c[step, a].astype(jnp.float32)

        @pl.when(hop < outer)
        def _():
            send_d[hop] = total.astype(jnp.bfloat16)
            d_copy(hop).start()

        @pl.when(hop == outer)
        def _():
            own_c[a] = total

    total = own_c[my_a]
    for hop in range(1, outer):
        d_copy(hop).wait_recv()
        total = total + recv_d[hop].astype(jnp.float32)
    share_b[0] = total.astype(jnp.bfloat16)
    for step in range(1, n_dp):
        b_copy(step).start()
    for step in range(1, n_dp):
        b_copy(step).wait_recv()
    total = jnp.zeros((blk, blk), jnp.float32)
    for group in range(n_dp):
        total = total + share_b[(dp - group + n_dp) % n_dp].astype(jnp.float32)
    scale = (blk * n_dp * n_f) ** (-0.5)
    total = total * scale
    grad_out[0] = total
    score = jnp.sqrt(jnp.sum(total * total, keepdims=True) * (1.0 / (blk * blk)) + 1e-06)
    score_out[0] = score[0, 0]

    @pl.loop(1, n_f)
    def _(step):
        meta_copy(step).wait_send()

    @pl.loop(0, outer)
    def _(a):
        @pl.loop(0, inner)
        def _(b):
            forwards(a, b, lambda copy: copy.wait_send())
            a_copy(a, b).wait_send()

        for step in range(1, inner):
            c_copy(a, step).wait_send()

    for hop in range(1, outer):
        d_copy(hop).wait_send()
    for step in range(1, n_dp):
        b_copy(step).wait_send()


def per_device(
    n_dp, n_f,
    tokens, out_grad, block_values, active_blocks, drop_slots, cand_blocks, group_counts
):
    rows, _ = tokens.shape
    stored, blk, _ = block_values.shape
    n_cand = cand_blocks.shape[0]
    outer = 4
    inner = n_f // (2 * outer)
    kept = stored - 1
    bf16, f32, i32 = jnp.bfloat16, jnp.float32, jnp.int32
    half = n_cand // 2
    sem = pltpu.SemaphoreType.DMA
    return pl.pallas_call(
        functools.partial(kernel, (n_dp, n_f, outer, inner)),
        out_shape=(
            jax.ShapeDtypeStruct((1, blk, blk), f32),
            jax.ShapeDtypeStruct((1,), f32),
        ),
        in_specs=[pl.BlockSpec(memory_space=pl.ANY)] * 3
        + [pl.BlockSpec(memory_space=pltpu.SMEM)] * 4,
        out_specs=(
            pl.BlockSpec(memory_space=pltpu.VMEM),
            pl.BlockSpec(memory_space=pltpu.SMEM),
        ),
        scratch_shapes=[
            pltpu.VMEM((tokens.shape[1] // blk, rows, blk), bf16),
            pltpu.VMEM((out_grad.shape[1] // blk, rows, blk), bf16),
            pltpu.VMEM(block_values.shape, bf16),
            pltpu.VMEM((n_f, kept * blk, blk), bf16),
            pltpu.VMEM((n_f, 1, 128), i32),
            pltpu.SMEM((n_f, 1, 128), i32),
            pltpu.VMEM((n_cand, blk, rows), bf16),
            pltpu.VMEM((kept, rows, blk), f32),
            pltpu.VMEM((n_cand, rows, blk), f32),
            pltpu.VMEM((half, blk, blk), bf16),
            pltpu.VMEM((half, blk, blk), bf16),
            pltpu.VMEM((blk, blk), f32),
            pltpu.VMEM((inner, outer, blk, blk), bf16),
            pltpu.VMEM((inner, outer, blk, blk), bf16),
            pltpu.VMEM((outer, blk, blk), f32),
            pltpu.VMEM((outer, blk, blk), bf16),
            pltpu.VMEM((outer, blk, blk), bf16),
            pltpu.VMEM((n_dp, blk, blk), bf16),
            sem((3,)), sem((n_f,)), sem((n_f,)), sem(()), sem((5, n_f)), sem((n_f,)),
            sem((half,)), sem((half,)), sem((inner, outer)), sem((inner, outer)),
            sem((outer,)), sem((outer,)), sem((n_dp,)), sem((n_dp,)),
        ],
        compiler_params=pltpu.CompilerParams(
            collective_id=0, has_side_effects=True, vmem_limit_bytes=48 * 1024 * 1024
        ),
        cost_estimate=pl.CostEstimate(
            flops=2 * blk ** 3 * (n_f * kept + n_cand),
            bytes_accessed=2 * (tokens.size + out_grad.size),
            transcendentals=n_cand * blk * blk,
        ),
    )(tokens, out_grad, block_values, active_blocks, drop_slots, cand_blocks, group_counts)


def solution(mesh):
    return jax.shard_map(
        functools.partial(per_device, mesh.shape["dp"], mesh.shape["fsdp"]),
        mesh=mesh,
        in_specs=(
            P(("dp", "fsdp"), None),
            P(("dp", "fsdp"), None),
            P("fsdp", None, None),
            P("fsdp", None),
            P("fsdp"),
            P(),
            P("dp"),
        ),
        out_specs=(P("fsdp", None, None), P("fsdp")),
        check_vma=False,
    )
```

```python
import functools
import jax
import jax.numpy as jnp
from jax import lax
from jax.experimental import pallas as pl
from jax.experimental.pallas import tpu as pltpu
from jax.sharding import PartitionSpec as P

MESH = pl.DeviceIdType.MESH


def gelu_slope(value_in):
    normal_cdf = 0.5 * (1.0 + lax.erf(value_in * 0.7071067811865476))
    density = jnp.exp(-0.5 * value_in * value_in) * 0.3989422804014327
    return normal_cdf + value_in * density


def kernel(
    dims,
    tok_hbm, og_hbm, bv_hbm, active, drops, cands, counts,
    grad_out, score_out,
    tok, og, bv, gath, meta_v, meta_s, xt, prod, acc,
    send_a, recv_a, own_a, send_c, recv_c, own_c, send_d, recv_d, share_b,
    load_sem, meta_send, meta_recv, meta_load, chunk_send, chunk_recv,
    a_send, a_recv, c_send, c_recv, d_send, d_recv, b_send, b_recv,
):
    n_dp, n_f, outer, inner = dims
    blk = bv.shape[1]
    stored = bv.shape[0]
    kept = stored - 1
    n_cand = acc.shape[0]
    dp = lax.axis_index("dp")
    me = lax.axis_index("fsdp")
    core = me % 2
    my_b = (me // 2) % inner
    my_a = me // (2 * inner)
    sibling = me + 1 - 2 * core

    def index(a, b, c):
        return (a * inner + b) * 2 + c

    load_bv = pltpu.make_async_copy(bv_hbm, bv, load_sem.at[0])
    load_bv.start()

    def load_columns(hbm, held, sem):
        @pl.loop(0, held.shape[0])
        def _(at):
            column = pl.multiple_of(at * blk, blk)
            pltpu.make_async_copy(hbm.at[:, pl.ds(column, blk)], held.at[at], sem).start()

    def wait_columns(held, sem):
        pltpu.make_async_copy(held, held, sem).wait()

    barrier = pltpu.get_barrier_semaphore()

    @pl.loop(1, n_f)
    def _(step):
        pl.semaphore_signal(
            barrier, inc=1, device_id={"fsdp": (me + step) % n_f}, device_id_type=MESH
        )

    @pl.loop(1, n_dp)
    def _(step):
        pl.semaphore_signal(
            barrier, inc=1, device_id={"dp": (dp + step) % n_dp}, device_id_type=MESH
        )

    load_columns(tok_hbm, tok, load_sem.at[1])
    drop = drops[0]
    lane = lax.broadcasted_iota(jnp.int32, (1, 128), 1)
    places = jnp.zeros((1, 128), jnp.int32)
    load_bv.wait()
    for slot in range(kept):
        at = slot + jnp.where(drop <= slot, 1, 0)
        gath[me, slot * blk:(slot + 1) * blk, :] = bv[at]
        places = jnp.where(lane == 2 * slot, active[0, at], places)
        places = jnp.where(lane == 2 * slot + 1, active[1, at], places)
    meta_v[me] = places

    pl.semaphore_wait(barrier, n_f - 1 + n_dp - 1)

    def chunk_copy(source, way, target):
        return pltpu.make_async_remote_copy(
            src_ref=gath.at[source],
            dst_ref=gath.at[source],
            send_sem=chunk_send.at[way, source],
            recv_sem=chunk_recv.at[source],
            device_id={"fsdp": target},
            device_id_type=MESH,
        )

    def meta_copy(step):
        target = (me + step) % n_f
        return pltpu.make_async_remote_copy(
            src_ref=meta_v.at[me],
            dst_ref=meta_v.at[me],
            send_sem=meta_send.at[step],
            recv_sem=meta_recv.at[me],
            device_id={"fsdp": target},
            device_id_type=MESH,
        )

    def meta_arrival(source):
        return pltpu.make_async_remote_copy(
            src_ref=meta_v.at[source],
            dst_ref=meta_v.at[source],
            send_sem=meta_send.at[0],
            recv_sem=meta_recv.at[source],
            device_id={"fsdp": sibling},
            device_id_type=MESH,
        )

    def forwards(a, b, act):
        source = index(a, b, core)

        @pl.when((b == my_b) & (a >= my_a) & (my_a > 0))
        def _():
            act(chunk_copy(source, 0, index(my_a - 1, my_b, core)))

        @pl.when((b == my_b) & (a <= my_a) & (my_a < outer - 1))
        def _():
            act(chunk_copy(source, 1, index(my_a + 1, my_b, core)))

        @pl.when((b >= my_b) & (my_b > 0))
        def _():
            act(chunk_copy(source, 2, index(my_a, my_b - 1, core)))

        @pl.when((b <= my_b) & (my_b < inner - 1))
        def _():
            act(chunk_copy(source, 3, index(my_a, my_b + 1, core)))

        act(chunk_copy(source, 4, sibling))

    def around(step, mine):
        return mine + (1 - 2 * (step % 2)) * ((step + 1) // 2)

    @pl.loop(1, n_f)
    def _(step):
        meta_copy(step).start()

    forwards(my_a, my_b, lambda copy: copy.start())
    load_columns(og_hbm, og, load_sem.at[2])
    wait_columns(tok, load_sem.at[1])
    acc[...] = jnp.zeros(acc.shape, jnp.float32)

    @pl.loop(1, n_f)
    def _(step):
        meta_arrival((me + step) % n_f).wait_recv()

    to_scalars = pltpu.make_async_copy(meta_v, meta_s, meta_load)
    to_scalars.start()
    to_scalars.wait()

    def process(source):
        for slot in range(kept):
            prod[slot] = jnp.dot(
                tok[meta_s[source, 0, 2 * slot]],
                gath[source, slot * blk:(slot + 1) * blk, :],
                preferred_element_type=jnp.float32,
            )
        columns = [meta_s[source, 0, 2 * slot + 1] for slot in range(kept)]
        for top in range(0, blk, 64):
            part = [prod[slot, top:top + 64, :] for slot in range(kept)]

            @pl.loop(0, n_cand // 16)
            def _(group):
                for at in range(16):
                    c = group * 16 + at
                    column = cands[1, c]
                    total = acc[c, top:top + 64, :]
                    for slot in range(kept):
                        chosen = jnp.where(columns[slot] == column, 1.0, 0.0)
                        total = total + chosen * part[slot]
                    acc[c, top:top + 64, :] = total

    turned = n_cand // (outer * inner)

    @pl.loop(0, 2 * outer - 1)
    def _(i):
        a = around(i, my_a)

        @pl.loop(0, 2 * inner - 1)
        def _(j):
            b = around(j, my_b)

            @pl.when((a >= 0) & (a < outer) & (b >= 0) & (b < inner))
            def _():
                @pl.when(i + j > 0)
                def _():
                    chunk_copy(index(a, b, core), 4, sibling).wait_recv()
                    forwards(a, b, lambda copy: copy.start())

                for at in range(turned):
                    c = (a * inner + b) * turned + at
                    xt[c] = tok[cands[0, c]].T

                @pl.loop(0, 2)
                def _(turn):
                    source = index(a, b, (core + turn) % 2)

                    @pl.when(turn == 1)
                    def _():
                        chunk_copy(source, 4, sibling).wait_recv()

                    process(source)

    wait_columns(og, load_sem.at[2])
    position = me * blk + lax.broadcasted_iota(jnp.int32, (blk, 1), 0)
    usable = jnp.where(position < counts[0], 1.0, 0.0)

    def term(c):
        slope = gelu_slope(acc[c])
        pre_grad = og[cands[1, c]].astype(jnp.float32) * slope * usable
        return jnp.dot(xt[c], pre_grad.astype(jnp.bfloat16), preferred_element_type=jnp.float32)

    def a_copy(a, b):
        at = a * inner + b
        return pltpu.make_async_remote_copy(
            src_ref=send_a.at[at], dst_ref=recv_a.at[at],
            send_sem=a_send.at[at], recv_sem=a_recv.at[at],
            device_id={"fsdp": sibling}, device_id_type=MESH,
        )

    def c_copy(a, step):
        return pltpu.make_async_remote_copy(
            src_ref=send_c.at[step, a], dst_ref=recv_c.at[step, a],
            send_sem=c_send.at[step, a], recv_sem=c_recv.at[step, a],
            device_id={"fsdp": index(my_a, (my_b + step) % inner, core)}, device_id_type=MESH,
        )

    def d_copy(step):
        return pltpu.make_async_remote_copy(
            src_ref=send_d.at[step], dst_ref=recv_d.at[step],
            send_sem=d_send.at[step], recv_sem=d_recv.at[step],
            device_id={"fsdp": index((my_a + step) % outer, my_b, core)}, device_id_type=MESH,
        )

    def b_copy(step):
        return pltpu.make_async_remote_copy(
            src_ref=share_b.at[0], dst_ref=share_b.at[step],
            send_sem=b_send.at[step], recv_sem=b_recv.at[step],
            device_id={"dp": (dp + step) % n_dp}, device_id_type=MESH,
        )

    def every(act):
        @pl.loop(1, inner + 1)
        def _(step):
            b = (my_b + step) % inner

            @pl.loop(0, outer // 2)
            def _(pair):
                act(step, b, [(my_a + 2 * pair + hop) % outer for hop in (1, 2)])

    def for_sibling(step, b, pair):
        found = [term(index(a, b, 1 - core)) for a in pair]
        for a, value in zip(pair, found):
            send_a[a * inner + b] = value.astype(jnp.bfloat16)
            a_copy(a, b).start()

    every(for_sibling)

    def for_mine(step, b, pair):
        found = [term(index(a, b, core)) for a in pair]
        for at, value in enumerate(found):
            own_a[at] = value
        for at, a in enumerate(pair):
            a_copy(a, b).wait_recv()
            total = own_a[at] + recv_a[a * inner + b].astype(jnp.float32)

            @pl.when(step < inner)
            def _():
                send_c[step, a] = total.astype(jnp.bfloat16)
                c_copy(a, step).start()

            @pl.when(step == inner)
            def _():
                own_c[a] = total

    every(for_mine)

    @pl.loop(1, outer + 1)
    def _(hop):
        a = (my_a + hop) % outer
        total = own_c[a]
        for step in range(1, inner):
            c_copy(a, step).wait_recv()
            total = total + recv_c[step, a].astype(jnp.float32)

        @pl.when(hop < outer)
        def _():
            send_d[hop] = total.astype(jnp.bfloat16)
            d_copy(hop).start()

        @pl.when(hop == outer)
        def _():
            own_c[a] = total

    total = own_c[my_a]
    for hop in range(1, outer):
        d_copy(hop).wait_recv()
        total = total + recv_d[hop].astype(jnp.float32)
    share_b[0] = total.astype(jnp.bfloat16)
    for step in range(1, n_dp):
        b_copy(step).start()
    for step in range(1, n_dp):
        b_copy(step).wait_recv()
    total = jnp.zeros((blk, blk), jnp.float32)
    for group in range(n_dp):
        total = total + share_b[(dp - group + n_dp) % n_dp].astype(jnp.float32)
    scale = (blk * n_dp * n_f) ** (-0.5)
    total = total * scale
    grad_out[0] = total
    score = jnp.sqrt(jnp.sum(total * total, keepdims=True) * (1.0 / (blk * blk)) + 1e-06)
    score_out[0] = score[0, 0]

    @pl.loop(1, n_f)
    def _(step):
        meta_copy(step).wait_send()

    @pl.loop(0, outer)
    def _(a):
        @pl.loop(0, inner)
        def _(b):
            forwards(a, b, lambda copy: copy.wait_send())
            a_copy(a, b).wait_send()

        for step in range(1, inner):
            c_copy(a, step).wait_send()

    for hop in range(1, outer):
        d_copy(hop).wait_send()
    for step in range(1, n_dp):
        b_copy(step).wait_send()


def per_device(
    n_dp, n_f,
    tokens, out_grad, block_values, active_blocks, drop_slots, cand_blocks, group_counts
):
    rows, _ = tokens.shape
    stored, blk, _ = block_values.shape
    n_cand = cand_blocks.shape[0]
    outer = 4
    inner = n_f // (2 * outer)
    kept = stored - 1
    bf16, f32, i32 = jnp.bfloat16, jnp.float32, jnp.int32
    half = n_cand // 2
    sem = pltpu.SemaphoreType.DMA
    return pl.pallas_call(
        functools.partial(kernel, (n_dp, n_f, outer, inner)),
        out_shape=(
            jax.ShapeDtypeStruct((1, blk, blk), f32),
            jax.ShapeDtypeStruct((1,), f32),
        ),
        in_specs=[pl.BlockSpec(memory_space=pl.ANY)] * 3
        + [pl.BlockSpec(memory_space=pltpu.SMEM)] * 4,
        out_specs=(
            pl.BlockSpec(memory_space=pltpu.VMEM),
            pl.BlockSpec(memory_space=pltpu.SMEM),
        ),
        scratch_shapes=[
            pltpu.VMEM((tokens.shape[1] // blk, rows, blk), bf16),
            pltpu.VMEM((out_grad.shape[1] // blk, rows, blk), bf16),
            pltpu.VMEM(block_values.shape, bf16),
            pltpu.VMEM((n_f, kept * blk, blk), bf16),
            pltpu.VMEM((n_f, 1, 128), i32),
            pltpu.SMEM((n_f, 1, 128), i32),
            pltpu.VMEM((n_cand, blk, rows), bf16),
            pltpu.VMEM((kept, rows, blk), f32),
            pltpu.VMEM((n_cand, rows, blk), f32),
            pltpu.VMEM((half, blk, blk), bf16),
            pltpu.VMEM((half, blk, blk), bf16),
            pltpu.VMEM((2, blk, blk), f32),
            pltpu.VMEM((inner, outer, blk, blk), bf16),
            pltpu.VMEM((inner, outer, blk, blk), bf16),
            pltpu.VMEM((outer, blk, blk), f32),
            pltpu.VMEM((outer, blk, blk), bf16),
            pltpu.VMEM((outer, blk, blk), bf16),
            pltpu.VMEM((n_dp, blk, blk), bf16),
            sem((3,)), sem((n_f,)), sem((n_f,)), sem(()), sem((5, n_f)), sem((n_f,)),
            sem((half,)), sem((half,)), sem((inner, outer)), sem((inner, outer)),
            sem((outer,)), sem((outer,)), sem((n_dp,)), sem((n_dp,)),
        ],
        compiler_params=pltpu.CompilerParams(
            collective_id=0, has_side_effects=True, vmem_limit_bytes=64 * 1024 * 1024
        ),
        cost_estimate=pl.CostEstimate(
            flops=2 * blk ** 3 * (n_f * kept + n_cand),
            bytes_accessed=2 * (tokens.size + out_grad.size),
            transcendentals=n_cand * blk * blk,
        ),
    )(
        tokens, out_grad, block_values, active_blocks.T, drop_slots, cand_blocks.T, group_counts
    )


def solution(mesh):
    return jax.shard_map(
        functools.partial(per_device, mesh.shape["dp"], mesh.shape["fsdp"]),
        mesh=mesh,
        in_specs=(
            P(("dp", "fsdp"), None),
            P(("dp", "fsdp"), None),
            P("fsdp", None, None),
            P("fsdp", None),
            P("fsdp"),
            P(),
            P("dp"),
        ),
        out_specs=(P("fsdp", None, None), P("fsdp")),
        check_vma=False,
    )
```

```python
import functools
import jax
import jax.numpy as jnp
from jax import lax
from jax.experimental import pallas as pl
from jax.experimental.pallas import tpu as pltpu
from jax.sharding import PartitionSpec as P

MESH = pl.DeviceIdType.MESH


def gelu_slope(value_in):
    normal_cdf = 0.5 * (1.0 + lax.erf(value_in * 0.7071067811865476))
    density = jnp.exp(-0.5 * value_in * value_in) * 0.3989422804014327
    return normal_cdf + value_in * density


def kernel(
    dims,
    tok_hbm, og_hbm, bv_hbm, active, drops, cands, counts,
    grad_out, score_out,
    tok, og, bv, gath, meta_v, meta_s, xt, prod, acc,
    send_a, recv_a, own_a, send_c, recv_c, own_c, send_d, recv_d, share_b,
    load_sem, meta_send, meta_recv, meta_load, chunk_send, chunk_recv,
    a_send, a_recv, c_send, c_recv, d_send, d_recv, b_send, b_recv,
):
    n_dp, n_f, outer, inner = dims
    blk = bv.shape[1]
    stored = bv.shape[0]
    kept = stored - 1
    half_slots = kept // 2
    n_cand = acc.shape[0]
    dp = lax.axis_index("dp")
    me = lax.axis_index("fsdp")
    core = me % 2
    my_b = (me // 2) % inner
    my_a = me // (2 * inner)
    sibling = me + 1 - 2 * core

    def index(a, b, c):
        return (a * inner + b) * 2 + c

    load_bv = pltpu.make_async_copy(bv_hbm, bv, load_sem.at[0])
    load_bv.start()

    def load_columns(hbm, held, sem, part, parts):
        share = pl.cdiv(held.shape[0], parts)

        @pl.loop(0, share)
        def _(step):
            at = part * share + step

            @pl.when(at < held.shape[0])
            def _():
                column = pl.multiple_of(at * blk, blk)
                pltpu.make_async_copy(hbm.at[:, pl.ds(column, blk)], held.at[at], sem).start()

    def wait_columns(held, sem):
        pltpu.make_async_copy(held, held, sem).wait()

    barrier = pltpu.get_barrier_semaphore()

    @pl.loop(1, n_f)
    def _(step):
        pl.semaphore_signal(
            barrier, inc=1, device_id={"fsdp": (me + step) % n_f}, device_id_type=MESH
        )

    @pl.loop(1, n_dp)
    def _(step):
        pl.semaphore_signal(
            barrier, inc=1, device_id={"dp": (dp + step) % n_dp}, device_id_type=MESH
        )

    load_columns(tok_hbm, tok, load_sem.at[1], 0, 1)
    drop = drops[0]
    lane = lax.broadcasted_iota(jnp.int32, (1, 128), 1)
    places = jnp.zeros((1, 128), jnp.int32)
    load_bv.wait()
    for slot in range(kept):
        at = slot + jnp.where(drop <= slot, 1, 0)
        held, place = slot // half_slots, slot % half_slots
        gath[me, held, place * blk:(place + 1) * blk, :] = bv[at]
        places = jnp.where(lane == 2 * slot, active[0, at], places)
        places = jnp.where(lane == 2 * slot + 1, active[1, at], places)
    meta_v[me] = places

    pl.semaphore_wait(barrier, n_f - 1 + n_dp - 1)

    mine = dp % 2
    partner = dp + 1 - 2 * mine

    def chunk_copy(source, way, target):
        return pltpu.make_async_remote_copy(
            src_ref=gath.at[source],
            dst_ref=gath.at[source],
            send_sem=chunk_send.at[way, source],
            recv_sem=chunk_recv.at[2, source],
            device_id={"fsdp": target},
            device_id_type=MESH,
        )

    def half_copy(source, half, way, device):
        return pltpu.make_async_remote_copy(
            src_ref=gath.at[source, half],
            dst_ref=gath.at[source, half],
            send_sem=chunk_send.at[way, source],
            recv_sem=chunk_recv.at[half, source],
            device_id=device,
            device_id_type=MESH,
        )

    def meta_copy(step):
        target = (me + step) % n_f
        return pltpu.make_async_remote_copy(
            src_ref=meta_v.at[me],
            dst_ref=meta_v.at[me],
            send_sem=meta_send.at[step],
            recv_sem=meta_recv.at[me],
            device_id={"fsdp": target},
            device_id_type=MESH,
        )

    def meta_arrival(source):
        return pltpu.make_async_remote_copy(
            src_ref=meta_v.at[source],
            dst_ref=meta_v.at[source],
            send_sem=meta_send.at[0],
            recv_sem=meta_recv.at[source],
            device_id={"fsdp": sibling},
            device_id_type=MESH,
        )

    def along_outer(a, act):
        source = index(a, my_b, core)

        @pl.when((a >= my_a) & (my_a > 0))
        def _():
            act(chunk_copy(source, 0, index(my_a - 1, my_b, core)))

        @pl.when((a <= my_a) & (my_a < outer - 1))
        def _():
            act(chunk_copy(source, 1, index(my_a + 1, my_b, core)))

        act(chunk_copy(source, 4, sibling))

    def along_inner(a, b, act):
        source = index(a, b, core)

        @pl.when((b >= my_b) & (my_b > 0))
        def _():
            act(half_copy(source, mine, 2, {"fsdp": index(my_a, my_b - 1, core)}))

        @pl.when((b <= my_b) & (my_b < inner - 1))
        def _():
            act(half_copy(source, mine, 3, {"fsdp": index(my_a, my_b + 1, core)}))

    def across(a, b, act):
        source = index(a, b, core)
        act(half_copy(source, mine, 5, {"dp": partner}))
        act(half_copy(source, mine, 4, {"fsdp": sibling}))

    def last_half(a, b):
        return half_copy(index(a, b, core), 1 - mine, 6, {"fsdp": sibling})

    def around(step, centre):
        return centre + (1 - 2 * (step % 2)) * ((step + 1) // 2)

    @pl.loop(1, n_f)
    def _(step):
        meta_copy(step).start()

    along_inner(my_a, my_b, lambda copy: copy.start())
    along_outer(my_a, lambda copy: copy.start())
    wait_columns(tok, load_sem.at[1])
    acc[...] = jnp.zeros(acc.shape, jnp.float32)

    @pl.loop(1, n_f)
    def _(step):
        meta_arrival((me + step) % n_f).wait_recv()

    to_scalars = pltpu.make_async_copy(meta_v, meta_s, meta_load)
    to_scalars.start()
    to_scalars.wait()

    def process(source):
        for slot in range(kept):
            prod[slot] = jnp.dot(
                tok[meta_s[source, 0, 2 * slot]],
                gath[source, slot // half_slots, pl.ds(slot % half_slots * blk, blk), :],
                preferred_element_type=jnp.float32,
            )
        columns = [meta_s[source, 0, 2 * slot + 1] for slot in range(kept)]
        for top in range(0, blk, 64):
            part = [prod[slot, top:top + 64, :] for slot in range(kept)]

            @pl.loop(0, n_cand // 16)
            def _(group):
                for at in range(16):
                    c = group * 16 + at
                    column = cands[1, c]
                    total = acc[c, top:top + 64, :]
                    for slot in range(kept):
                        chosen = jnp.where(columns[slot] == column, 1.0, 0.0)
                        total = total + chosen * part[slot]
                    acc[c, top:top + 64, :] = total

    turned = n_cand // (outer * inner)

    @pl.loop(0, 2 * outer - 1)
    def _(i):
        a = around(i, my_a)

        @pl.loop(0, 2 * inner - 1)
        def _(j):
            b = around(j, my_b)

            @pl.when((a >= 0) & (a < outer) & (b >= 0) & (b < inner))
            def _():
                source = index(a, b, core)
                other = index(a, b, 1 - core)

                @pl.when((j == 0) & (i > 0))
                def _():
                    chunk_copy(source, 4, sibling).wait_recv()
                    along_outer(a, lambda copy: copy.start())
                    along_inner(a, b, lambda copy: copy.start())

                @pl.when(j > 0)
                def _():
                    half_copy(source, mine, 4, {"fsdp": sibling}).wait_recv()
                    across(a, b, lambda copy: copy.start())
                    along_inner(a, b, lambda copy: copy.start())
                    last_half(a, b).wait_recv()
                    last_half(a, b).start()

                load_columns(og_hbm, og, load_sem.at[2], a * inner + b, outer * inner)

                for at in range(turned):
                    c = (a * inner + b) * turned + at
                    xt[c] = tok[cands[0, c]].T

                @pl.loop(0, 2)
                def _(turn):
                    source = index(a, b, (core + turn) % 2)

                    @pl.when((turn == 1) & (j == 0))
                    def _():
                        chunk_copy(other, 4, sibling).wait_recv()

                    @pl.when((turn == 1) & (j > 0))
                    def _():
                        half_copy(other, 0, 4, {"fsdp": sibling}).wait_recv()
                        half_copy(other, 1, 4, {"fsdp": sibling}).wait_recv()

                    process(source)

    wait_columns(og, load_sem.at[2])
    position = me * blk + lax.broadcasted_iota(jnp.int32, (blk, 1), 0)
    usable = jnp.where(position < counts[0], 1.0, 0.0)

    def term(c):
        slope = gelu_slope(acc[c])
        pre_grad = og[cands[1, c]].astype(jnp.float32) * slope * usable
        return jnp.dot(xt[c], pre_grad.astype(jnp.bfloat16), preferred_element_type=jnp.float32)

    def a_copy(a, b):
        at = a * inner + b
        return pltpu.make_async_remote_copy(
            src_ref=send_a.at[at], dst_ref=recv_a.at[at],
            send_sem=a_send.at[at], recv_sem=a_recv.at[at],
            device_id={"fsdp": sibling}, device_id_type=MESH,
        )

    def c_copy(a, step):
        return pltpu.make_async_remote_copy(
            src_ref=send_c.at[step, a], dst_ref=recv_c.at[step, a],
            send_sem=c_send.at[step, a], recv_sem=c_recv.at[step, a],
            device_id={"fsdp": index(my_a, (my_b + step) % inner, core)}, device_id_type=MESH,
        )

    def d_copy(step):
        return pltpu.make_async_remote_copy(
            src_ref=send_d.at[step], dst_ref=recv_d.at[step],
            send_sem=d_send.at[step], recv_sem=d_recv.at[step],
            device_id={"fsdp": index((my_a + step) % outer, my_b, core)}, device_id_type=MESH,
        )

    def b_copy(step):
        return pltpu.make_async_remote_copy(
            src_ref=share_b.at[0], dst_ref=share_b.at[step],
            send_sem=b_send.at[step], recv_sem=b_recv.at[step],
            device_id={"dp": (dp + step) % n_dp}, device_id_type=MESH,
        )

    def every(act):
        @pl.loop(1, inner + 1)
        def _(step):
            b = (my_b + step) % inner

            @pl.loop(0, outer // 2)
            def _(pair):
                act(step, b, [(my_a + 2 * pair + hop) % outer for hop in (1, 2)])

    def for_sibling(step, b, pair):
        found = [term(index(a, b, 1 - core)) for a in pair]
        for a, value in zip(pair, found):
            send_a[a * inner + b] = value.astype(jnp.bfloat16)
            a_copy(a, b).start()

    every(for_sibling)

    def for_mine(step, b, pair):
        found = [term(index(a, b, core)) for a in pair]
        for at, value in enumerate(found):
            own_a[at] = value
        for at, a in enumerate(pair):
            a_copy(a, b).wait_recv()
            total = own_a[at] + recv_a[a * inner + b].astype(jnp.float32)

            @pl.when(step < inner)
            def _():
                send_c[step, a] = total.astype(jnp.bfloat16)
                c_copy(a, step).start()

            @pl.when(step == inner)
            def _():
                own_c[a] = total

    every(for_mine)

    @pl.loop(1, outer + 1)
    def _(hop):
        a = (my_a + hop) % outer
        total = own_c[a]
        for step in range(1, inner):
            c_copy(a, step).wait_recv()
            total = total + recv_c[step, a].astype(jnp.float32)

        @pl.when(hop < outer)
        def _():
            send_d[hop] = total.astype(jnp.bfloat16)
            d_copy(hop).start()

        @pl.when(hop == outer)
        def _():
            own_c[a] = total

    total = own_c[my_a]
    for hop in range(1, outer):
        d_copy(hop).wait_recv()
        total = total + recv_d[hop].astype(jnp.float32)
    share_b[0] = total.astype(jnp.bfloat16)
    for step in range(1, n_dp):
        b_copy(step).start()
    for step in range(1, n_dp):
        b_copy(step).wait_recv()
    total = jnp.zeros((blk, blk), jnp.float32)
    for group in range(n_dp):
        total = total + share_b[(dp - group + n_dp) % n_dp].astype(jnp.float32)
    scale = (blk * n_dp * n_f) ** (-0.5)
    total = total * scale
    grad_out[0] = total
    score = jnp.sqrt(jnp.sum(total * total, keepdims=True) * (1.0 / (blk * blk)) + 1e-06)
    score_out[0] = score[0, 0]

    @pl.loop(1, n_f)
    def _(step):
        meta_copy(step).wait_send()

    @pl.loop(0, outer)
    def _(a):
        @pl.loop(0, inner)
        def _(b):
            along_inner(a, b, lambda copy: copy.wait_send())
            a_copy(a, b).wait_send()

            @pl.when(b == my_b)
            def _():
                along_outer(a, lambda copy: copy.wait_send())

            @pl.when(b != my_b)
            def _():
                across(a, b, lambda copy: copy.wait_send())
                last_half(a, b).wait_send()

        for step in range(1, inner):
            c_copy(a, step).wait_send()

    for hop in range(1, outer):
        d_copy(hop).wait_send()
    for step in range(1, n_dp):
        b_copy(step).wait_send()


def per_device(
    n_dp, n_f,
    tokens, out_grad, block_values, active_blocks, drop_slots, cand_blocks, group_counts
):
    rows, _ = tokens.shape
    stored, blk, _ = block_values.shape
    n_cand = cand_blocks.shape[0]
    outer = 4
    inner = n_f // (2 * outer)
    kept = stored - 1
    bf16, f32, i32 = jnp.bfloat16, jnp.float32, jnp.int32
    half = n_cand // 2
    sem = pltpu.SemaphoreType.DMA
    return pl.pallas_call(
        functools.partial(kernel, (n_dp, n_f, outer, inner)),
        out_shape=(
            jax.ShapeDtypeStruct((1, blk, blk), f32),
            jax.ShapeDtypeStruct((1,), f32),
        ),
        in_specs=[pl.BlockSpec(memory_space=pl.ANY)] * 3
        + [pl.BlockSpec(memory_space=pltpu.SMEM)] * 4,
        out_specs=(
            pl.BlockSpec(memory_space=pltpu.VMEM),
            pl.BlockSpec(memory_space=pltpu.SMEM),
        ),
        scratch_shapes=[
            pltpu.VMEM((tokens.shape[1] // blk, rows, blk), bf16),
            pltpu.VMEM((out_grad.shape[1] // blk, rows, blk), bf16),
            pltpu.VMEM(block_values.shape, bf16),
            pltpu.VMEM((n_f, 2, kept // 2 * blk, blk), bf16),
            pltpu.VMEM((n_f, 1, 128), i32),
            pltpu.SMEM((n_f, 1, 128), i32),
            pltpu.VMEM((n_cand, blk, rows), bf16),
            pltpu.VMEM((kept, rows, blk), f32),
            pltpu.VMEM((n_cand, rows, blk), f32),
            pltpu.VMEM((half, blk, blk), bf16),
            pltpu.VMEM((half, blk, blk), bf16),
            pltpu.VMEM((2, blk, blk), f32),
            pltpu.VMEM((inner, outer, blk, blk), bf16),
            pltpu.VMEM((inner, outer, blk, blk), bf16),
            pltpu.VMEM((outer, blk, blk), f32),
            pltpu.VMEM((outer, blk, blk), bf16),
            pltpu.VMEM((outer, blk, blk), bf16),
            pltpu.VMEM((n_dp, blk, blk), bf16),
            sem((3,)), sem((n_f,)), sem((n_f,)), sem(()), sem((7, n_f)), sem((3, n_f)),
            sem((half,)), sem((half,)), sem((inner, outer)), sem((inner, outer)),
            sem((outer,)), sem((outer,)), sem((n_dp,)), sem((n_dp,)),
        ],
        compiler_params=pltpu.CompilerParams(
            collective_id=0, has_side_effects=True, vmem_limit_bytes=64 * 1024 * 1024
        ),
        cost_estimate=pl.CostEstimate(
            flops=2 * blk ** 3 * (n_f * kept + n_cand),
            bytes_accessed=2 * (tokens.size + out_grad.size),
            transcendentals=n_cand * blk * blk,
        ),
    )(
        tokens, out_grad, block_values, active_blocks.T, drop_slots, cand_blocks.T, group_counts
    )


def solution(mesh):
    return jax.shard_map(
        functools.partial(per_device, mesh.shape["dp"], mesh.shape["fsdp"]),
        mesh=mesh,
        in_specs=(
            P(("dp", "fsdp"), None),
            P(("dp", "fsdp"), None),
            P("fsdp", None, None),
            P("fsdp", None),
            P("fsdp"),
            P(),
            P("dp"),
        ),
        out_specs=(P("fsdp", None, None), P("fsdp")),
        check_vma=False,
    )
```

```python
import functools
import jax
import jax.numpy as jnp
from jax import lax
from jax.experimental import pallas as pl
from jax.experimental.pallas import tpu as pltpu
from jax.sharding import PartitionSpec as P

MESH = pl.DeviceIdType.MESH


def gelu_slope(value_in):
    normal_cdf = 0.5 * (1.0 + lax.erf(value_in * 0.7071067811865476))
    density = jnp.exp(-0.5 * value_in * value_in) * 0.3989422804014327
    return normal_cdf + value_in * density


def kernel(
    dims,
    tok_hbm, og_hbm, bv_hbm, active, drops, cands, counts,
    grad_out, score_out,
    tok, og, bv, gath, meta_v, meta_s, xt, prod, acc,
    send_a, recv_a, own_a, send_c, recv_c, own_c, send_d, recv_d, share_b,
    load_sem, meta_send, meta_recv, meta_load, chunk_send, chunk_recv,
    a_send, a_recv, c_send, c_recv, d_send, d_recv, b_send, b_recv,
):
    n_dp, n_f, outer, inner = dims
    blk = bv.shape[1]
    stored = bv.shape[0]
    kept = stored - 1
    n_cand = acc.shape[0]
    dp = lax.axis_index("dp")
    me = lax.axis_index("fsdp")
    core = me % 2
    my_b = (me // 2) % inner
    my_a = me // (2 * inner)
    sibling = me + 1 - 2 * core

    def index(a, b, c):
        return (a * inner + b) * 2 + c

    load_bv = pltpu.make_async_copy(bv_hbm, bv, load_sem.at[0])
    load_bv.start()

    def load_columns(hbm, held, sem):
        @pl.loop(0, held.shape[0])
        def _(at):
            column = pl.multiple_of(at * blk, blk)
            pltpu.make_async_copy(hbm.at[:, pl.ds(column, blk)], held.at[at], sem).start()

    def wait_columns(held, sem):
        pltpu.make_async_copy(held, held, sem).wait()

    barrier = pltpu.get_barrier_semaphore()

    @pl.loop(1, n_f)
    def _(step):
        pl.semaphore_signal(
            barrier, inc=1, device_id={"fsdp": (me + step) % n_f}, device_id_type=MESH
        )

    @pl.loop(1, n_dp)
    def _(step):
        pl.semaphore_signal(
            barrier, inc=1, device_id={"dp": (dp + step) % n_dp}, device_id_type=MESH
        )

    load_columns(tok_hbm, tok, load_sem.at[1])
    drop = drops[0]
    lane = lax.broadcasted_iota(jnp.int32, (1, 128), 1)
    places = jnp.zeros((1, 128), jnp.int32)
    load_bv.wait()
    for slot in range(kept):
        at = slot + jnp.where(drop <= slot, 1, 0)
        gath[me, slot * blk:(slot + 1) * blk, :] = bv[at]
        places = jnp.where(lane == 2 * slot, active[0, at], places)
        places = jnp.where(lane == 2 * slot + 1, active[1, at], places)
    meta_v[me] = places

    pl.semaphore_wait(barrier, n_f - 1 + n_dp - 1)

    def chunk_copy(source, way, target):
        return pltpu.make_async_remote_copy(
            src_ref=gath.at[source],
            dst_ref=gath.at[source],
            send_sem=chunk_send.at[way, source],
            recv_sem=chunk_recv.at[source],
            device_id={"fsdp": target},
            device_id_type=MESH,
        )

    def meta_copy(step):
        target = (me + step) % n_f
        return pltpu.make_async_remote_copy(
            src_ref=meta_v.at[me],
            dst_ref=meta_v.at[me],
            send_sem=meta_send.at[step],
            recv_sem=meta_recv.at[me],
            device_id={"fsdp": target},
            device_id_type=MESH,
        )

    def meta_arrival(source):
        return pltpu.make_async_remote_copy(
            src_ref=meta_v.at[source],
            dst_ref=meta_v.at[source],
            send_sem=meta_send.at[0],
            recv_sem=meta_recv.at[source],
            device_id={"fsdp": sibling},
            device_id_type=MESH,
        )

    def forwards(a, b, act):
        source = index(a, b, core)

        @pl.when((b == my_b) & (a >= my_a) & (my_a > 0))
        def _():
            act(chunk_copy(source, 0, index(my_a - 1, my_b, core)))

        @pl.when((b == my_b) & (a <= my_a) & (my_a < outer - 1))
        def _():
            act(chunk_copy(source, 1, index(my_a + 1, my_b, core)))

        @pl.when((b >= my_b) & (my_b > 0))
        def _():
            act(chunk_copy(source, 2, index(my_a, my_b - 1, core)))

        @pl.when((b <= my_b) & (my_b < inner - 1))
        def _():
            act(chunk_copy(source, 3, index(my_a, my_b + 1, core)))

        act(chunk_copy(source, 4, sibling))

    def around(step, mine):
        return mine + (1 - 2 * (step % 2)) * ((step + 1) // 2)

    @pl.loop(1, n_f)
    def _(step):
        meta_copy(step).start()

    forwards(my_a, my_b, lambda copy: copy.start())
    load_columns(og_hbm, og, load_sem.at[2])
    wait_columns(tok, load_sem.at[1])
    acc[...] = jnp.zeros(acc.shape, jnp.float32)

    @pl.loop(1, n_f)
    def _(step):
        meta_arrival((me + step) % n_f).wait_recv()

    to_scalars = pltpu.make_async_copy(meta_v, meta_s, meta_load)
    to_scalars.start()
    to_scalars.wait()

    def process(source):
        for slot in range(kept):
            prod[slot] = jnp.dot(
                tok[meta_s[source, 0, 2 * slot]],
                gath[source, slot * blk:(slot + 1) * blk, :],
                preferred_element_type=jnp.float32,
            )
        columns = [meta_s[source, 0, 2 * slot + 1] for slot in range(kept)]
        for top in range(0, blk, 64):
            part = [prod[slot, top:top + 64, :] for slot in range(kept)]

            @pl.loop(0, n_cand // 16)
            def _(group):
                for at in range(16):
                    c = group * 16 + at
                    column = cands[1, c]
                    total = acc[c, top:top + 64, :]
                    for slot in range(kept):
                        chosen = jnp.where(columns[slot] == column, 1.0, 0.0)
                        total = total + chosen * part[slot]
                    acc[c, top:top + 64, :] = total

    turned = n_cand // (outer * inner)

    steps = outer * inner

    def nearest(step, mine, size):
        ends = jnp.minimum(mine, size - 1 - mine)
        rest = jnp.where(mine < size - 1 - mine, step, size - 1 - step)
        return jnp.where(step <= 2 * ends, around(step, mine), rest)

    def place_at(step):
        return nearest(step // inner, my_a, outer), nearest(step % inner, my_b, inner)

    @pl.loop(0, steps + 1)
    def _(step):
        @pl.when((step > 0) & (step < steps))
        def _():
            a, b = place_at(step)
            chunk_copy(index(a, b, core), 4, sibling).wait_recv()
            forwards(a, b, lambda copy: copy.start())

        @pl.loop(0, 2)
        def _(turn):
            at = step - 1 + turn

            @pl.when((at >= 0) & (at < steps))
            def _():
                a, b = place_at(at)

                @pl.when(turn == 0)
                def _():
                    chunk_copy(index(a, b, 1 - core), 4, sibling).wait_recv()

                process(index(a, b, (core + 1 + turn) % 2))

        @pl.when(step < steps)
        def _():
            for at in range(turned):
                c = step * turned + at
                xt[c] = tok[cands[0, c]].T

    wait_columns(og, load_sem.at[2])
    position = me * blk + lax.broadcasted_iota(jnp.int32, (blk, 1), 0)
    usable = jnp.where(position < counts[0], 1.0, 0.0)

    def term(c):
        slope = gelu_slope(acc[c])
        pre_grad = og[cands[1, c]].astype(jnp.float32) * slope * usable
        return jnp.dot(xt[c], pre_grad.astype(jnp.bfloat16), preferred_element_type=jnp.float32)

    def a_copy(a, b):
        at = a * inner + b
        return pltpu.make_async_remote_copy(
            src_ref=send_a.at[at], dst_ref=recv_a.at[at],
            send_sem=a_send.at[at], recv_sem=a_recv.at[at],
            device_id={"fsdp": sibling}, device_id_type=MESH,
        )

    def c_copy(a, step):
        return pltpu.make_async_remote_copy(
            src_ref=send_c.at[step, a], dst_ref=recv_c.at[step, a],
            send_sem=c_send.at[step, a], recv_sem=c_recv.at[step, a],
            device_id={"fsdp": index(my_a, (my_b + step) % inner, core)}, device_id_type=MESH,
        )

    def d_copy(step):
        return pltpu.make_async_remote_copy(
            src_ref=send_d.at[step], dst_ref=recv_d.at[step],
            send_sem=d_send.at[step], recv_sem=d_recv.at[step],
            device_id={"fsdp": index((my_a + step) % outer, my_b, core)}, device_id_type=MESH,
        )

    def b_copy(step):
        return pltpu.make_async_remote_copy(
            src_ref=share_b.at[0], dst_ref=share_b.at[step],
            send_sem=b_send.at[step], recv_sem=b_recv.at[step],
            device_id={"dp": (dp + step) % n_dp}, device_id_type=MESH,
        )

    def every(act):
        @pl.loop(1, inner + 1)
        def _(step):
            b = (my_b + step) % inner

            @pl.loop(0, outer // 2)
            def _(pair):
                act(step, b, [(my_a + 2 * pair + hop) % outer for hop in (1, 2)])

    def for_sibling(step, b, pair):
        found = [term(index(a, b, 1 - core)) for a in pair]
        for a, value in zip(pair, found):
            send_a[a * inner + b] = value.astype(jnp.bfloat16)
            a_copy(a, b).start()

    every(for_sibling)

    def for_mine(step, b, pair):
        found = [term(index(a, b, core)) for a in pair]
        for at, value in enumerate(found):
            own_a[at] = value
        for at, a in enumerate(pair):
            a_copy(a, b).wait_recv()
            total = own_a[at] + recv_a[a * inner + b].astype(jnp.float32)

            @pl.when(step < inner)
            def _():
                send_c[step, a] = total.astype(jnp.bfloat16)
                c_copy(a, step).start()

            @pl.when(step == inner)
            def _():
                own_c[a] = total

    every(for_mine)

    @pl.loop(1, outer + 1)
    def _(hop):
        a = (my_a + hop) % outer
        total = own_c[a]
        for step in range(1, inner):
            c_copy(a, step).wait_recv()
            total = total + recv_c[step, a].astype(jnp.float32)

        @pl.when(hop < outer)
        def _():
            send_d[hop] = total.astype(jnp.bfloat16)
            d_copy(hop).start()

        @pl.when(hop == outer)
        def _():
            own_c[a] = total

    total = own_c[my_a]
    for hop in range(1, outer):
        d_copy(hop).wait_recv()
        total = total + recv_d[hop].astype(jnp.float32)
    share_b[0] = total.astype(jnp.bfloat16)
    for step in range(1, n_dp):
        b_copy(step).start()
    for step in range(1, n_dp):
        b_copy(step).wait_recv()
    total = jnp.zeros((blk, blk), jnp.float32)
    for group in range(n_dp):
        total = total + share_b[(dp - group + n_dp) % n_dp].astype(jnp.float32)
    scale = (blk * n_dp * n_f) ** (-0.5)
    total = total * scale
    grad_out[0] = total
    score = jnp.sqrt(jnp.sum(total * total, keepdims=True) * (1.0 / (blk * blk)) + 1e-06)
    score_out[0] = score[0, 0]

    @pl.loop(1, n_f)
    def _(step):
        meta_copy(step).wait_send()

    @pl.loop(0, outer)
    def _(a):
        @pl.loop(0, inner)
        def _(b):
            forwards(a, b, lambda copy: copy.wait_send())
            a_copy(a, b).wait_send()

        for step in range(1, inner):
            c_copy(a, step).wait_send()

    for hop in range(1, outer):
        d_copy(hop).wait_send()
    for step in range(1, n_dp):
        b_copy(step).wait_send()


def per_device(
    n_dp, n_f,
    tokens, out_grad, block_values, active_blocks, drop_slots, cand_blocks, group_counts
):
    rows, _ = tokens.shape
    stored, blk, _ = block_values.shape
    n_cand = cand_blocks.shape[0]
    outer = 4
    inner = n_f // (2 * outer)
    kept = stored - 1
    bf16, f32, i32 = jnp.bfloat16, jnp.float32, jnp.int32
    half = n_cand // 2
    sem = pltpu.SemaphoreType.DMA
    return pl.pallas_call(
        functools.partial(kernel, (n_dp, n_f, outer, inner)),
        out_shape=(
            jax.ShapeDtypeStruct((1, blk, blk), f32),
            jax.ShapeDtypeStruct((1,), f32),
        ),
        in_specs=[pl.BlockSpec(memory_space=pl.ANY)] * 3
        + [pl.BlockSpec(memory_space=pltpu.SMEM)] * 4,
        out_specs=(
            pl.BlockSpec(memory_space=pltpu.VMEM),
            pl.BlockSpec(memory_space=pltpu.SMEM),
        ),
        scratch_shapes=[
            pltpu.VMEM((tokens.shape[1] // blk, rows, blk), bf16),
            pltpu.VMEM((out_grad.shape[1] // blk, rows, blk), bf16),
            pltpu.VMEM(block_values.shape, bf16),
            pltpu.VMEM((n_f, kept * blk, blk), bf16),
            pltpu.VMEM((n_f, 1, 128), i32),
            pltpu.SMEM((n_f, 1, 128), i32),
            pltpu.VMEM((n_cand, blk, rows), bf16),
            pltpu.VMEM((kept, rows, blk), f32),
            pltpu.VMEM((n_cand, rows, blk), f32),
            pltpu.VMEM((half, blk, blk), bf16),
            pltpu.VMEM((half, blk, blk), bf16),
            pltpu.VMEM((2, blk, blk), f32),
            pltpu.VMEM((inner, outer, blk, blk), bf16),
            pltpu.VMEM((inner, outer, blk, blk), bf16),
            pltpu.VMEM((outer, blk, blk), f32),
            pltpu.VMEM((outer, blk, blk), bf16),
            pltpu.VMEM((outer, blk, blk), bf16),
            pltpu.VMEM((n_dp, blk, blk), bf16),
            sem((3,)), sem((n_f,)), sem((n_f,)), sem(()), sem((5, n_f)), sem((n_f,)),
            sem((half,)), sem((half,)), sem((inner, outer)), sem((inner, outer)),
            sem((outer,)), sem((outer,)), sem((n_dp,)), sem((n_dp,)),
        ],
        compiler_params=pltpu.CompilerParams(
            collective_id=0, has_side_effects=True, vmem_limit_bytes=64 * 1024 * 1024 - 128 * 1024
        ),
        cost_estimate=pl.CostEstimate(
            flops=2 * blk ** 3 * (n_f * kept + n_cand),
            bytes_accessed=2 * (tokens.size + out_grad.size),
            transcendentals=n_cand * blk * blk,
        ),
    )(
        tokens, out_grad, block_values, active_blocks.T, drop_slots, cand_blocks.T, group_counts
    )


def solution(mesh):
    return jax.shard_map(
        functools.partial(per_device, mesh.shape["dp"], mesh.shape["fsdp"]),
        mesh=mesh,
        in_specs=(
            P(("dp", "fsdp"), None),
            P(("dp", "fsdp"), None),
            P("fsdp", None, None),
            P("fsdp", None),
            P("fsdp"),
            P(),
            P("dp"),
        ),
        out_specs=(P("fsdp", None, None), P("fsdp")),
        check_vma=False,
    )
```

```python
import functools
import jax
import jax.numpy as jnp
from jax import lax
from jax.experimental import pallas as pl
from jax.experimental.pallas import tpu as pltpu
from jax.sharding import PartitionSpec as P

MESH = pl.DeviceIdType.MESH


def gelu_slope(value_in):
    normal_cdf = 0.5 * (1.0 + lax.erf(value_in * 0.7071067811865476))
    density = jnp.exp(-0.5 * value_in * value_in) * 0.3989422804014327
    return normal_cdf + value_in * density


def kernel(
    dims,
    tok_hbm, og_hbm, bv_hbm, active, drops, cands, counts,
    grad_out, score_out,
    tok, og, bv, gath, meta_v, meta_s, xt, sums, acc,
    send_a, recv_a, own_a, send_c, recv_c, own_c, send_d, recv_d,
    load_sem, meta_send, meta_recv, meta_load, chunk_send, chunk_recv,
    a_send, a_recv, c_send, c_recv, d_send, d_recv,
):
    n_dp, n_f, outer, inner = dims
    blk = bv.shape[1]
    stored = bv.shape[0]
    kept = stored - 1
    n_cand = acc.shape[0]
    dp = lax.axis_index("dp")
    me = lax.axis_index("fsdp")
    core = me % 2
    my_b = (me // 2) % inner
    my_a = me // (2 * inner)
    sibling = me + 1 - 2 * core

    def index(a, b, c):
        return (a * inner + b) * 2 + c

    load_bv = pltpu.make_async_copy(bv_hbm, bv, load_sem.at[0])
    load_bv.start()

    def load_columns(hbm, held, sem):
        @pl.loop(0, held.shape[0])
        def _(at):
            column = pl.multiple_of(at * blk, blk)
            pltpu.make_async_copy(hbm.at[:, pl.ds(column, blk)], held.at[at], sem).start()

    def wait_columns(held, sem):
        pltpu.make_async_copy(held, held, sem).wait()

    barrier = pltpu.get_barrier_semaphore()

    @pl.loop(1, n_f)
    def _(step):
        pl.semaphore_signal(
            barrier, inc=1, device_id={"fsdp": (me + step) % n_f}, device_id_type=MESH
        )

    @pl.loop(1, n_dp)
    def _(step):
        def greet(a, b):
            pl.semaphore_signal(
                barrier,
                inc=1,
                device_id={"dp": (dp + step) % n_dp, "fsdp": index(a, b, core)},
                device_id_type=MESH,
            )

        @pl.loop(0, inner)
        def _(b):
            greet(my_a, b)

        @pl.loop(1, outer)
        def _(hop):
            greet((my_a + hop) % outer, my_b)

    load_columns(tok_hbm, tok, load_sem.at[1])
    drop = drops[0]
    lane = lax.broadcasted_iota(jnp.int32, (1, 128), 1)
    places = jnp.zeros((1, 128), jnp.int32)
    load_bv.wait()
    for slot in range(kept):
        at = slot + jnp.where(drop <= slot, 1, 0)
        gath[me, slot * blk:(slot + 1) * blk, :] = bv[at]
        places = jnp.where(lane == 2 * slot, active[0, at], places)
        places = jnp.where(lane == 2 * slot + 1, active[1, at], places)
    meta_v[me] = places

    pl.semaphore_wait(barrier, n_f - 1 + (n_dp - 1) * (inner + outer - 1))

    def chunk_copy(source, way, target):
        return pltpu.make_async_remote_copy(
            src_ref=gath.at[source],
            dst_ref=gath.at[source],
            send_sem=chunk_send.at[way, source],
            recv_sem=chunk_recv.at[source],
            device_id={"fsdp": target},
            device_id_type=MESH,
        )

    def meta_copy(step):
        target = (me + step) % n_f
        return pltpu.make_async_remote_copy(
            src_ref=meta_v.at[me],
            dst_ref=meta_v.at[me],
            send_sem=meta_send.at[step],
            recv_sem=meta_recv.at[me],
            device_id={"fsdp": target},
            device_id_type=MESH,
        )

    def meta_arrival(source):
        return pltpu.make_async_remote_copy(
            src_ref=meta_v.at[source],
            dst_ref=meta_v.at[source],
            send_sem=meta_send.at[0],
            recv_sem=meta_recv.at[source],
            device_id={"fsdp": sibling},
            device_id_type=MESH,
        )

    def forwards(a, b, act):
        source = index(a, b, core)

        @pl.when((b == my_b) & (a >= my_a) & (my_a > 0))
        def _():
            act(chunk_copy(source, 0, index(my_a - 1, my_b, core)))

        @pl.when((b == my_b) & (a <= my_a) & (my_a < outer - 1))
        def _():
            act(chunk_copy(source, 1, index(my_a + 1, my_b, core)))

        @pl.when((b >= my_b) & (my_b > 0))
        def _():
            act(chunk_copy(source, 2, index(my_a, my_b - 1, core)))

        @pl.when((b <= my_b) & (my_b < inner - 1))
        def _():
            act(chunk_copy(source, 3, index(my_a, my_b + 1, core)))

        act(chunk_copy(source, 4, sibling))

    def around(step, mine):
        return mine + (1 - 2 * (step % 2)) * ((step + 1) // 2)

    @pl.loop(1, n_f)
    def _(step):
        meta_copy(step).start()

    forwards(my_a, my_b, lambda copy: copy.start())
    load_columns(og_hbm, og, load_sem.at[2])
    wait_columns(tok, load_sem.at[1])
    acc[...] = jnp.zeros(acc.shape, jnp.float32)

    @pl.loop(1, n_f)
    def _(step):
        meta_arrival((me + step) % n_f).wait_recv()

    to_scalars = pltpu.make_async_copy(meta_v, meta_s, meta_load)
    to_scalars.start()
    to_scalars.wait()

    for turn in range(2):
        sums[turn, 0] = jnp.zeros(sums.shape[2:], jnp.float32)

    def products(source, turn):
        for slot in range(kept):
            sums[turn, 1 << slot] = jnp.dot(
                tok[meta_s[source, 0, 2 * slot]],
                gath[source, slot * blk:(slot + 1) * blk, :],
                preferred_element_type=jnp.float32,
            )

        @pl.loop(0, blk // 32)
        def _(part):
            rows = pl.ds(pl.multiple_of(part * 32, 32), 32)
            found = [None] * (1 << kept)
            for slot in range(kept):
                found[1 << slot] = sums[turn, 1 << slot, rows, :]
                for low in range(1, 1 << slot):
                    found[low + (1 << slot)] = found[low] + found[1 << slot]
                    sums[turn, low + (1 << slot), rows, :] = found[low + (1 << slot)]

    def chosen(source, column, valid):
        bits = jnp.int32(0)
        for slot in range(kept):
            bits = bits + jnp.where(meta_s[source, 0, 2 * slot + 1] == column, 1 << slot, 0)
        return bits * valid

    turned = n_cand // (outer * inner)

    steps = outer * inner

    def nearest(step, mine, size):
        ends = jnp.minimum(mine, size - 1 - mine)
        rest = jnp.where(mine < size - 1 - mine, step, size - 1 - step)
        return jnp.where(step <= 2 * ends, around(step, mine), rest)

    def place_at(step):
        return nearest(step // inner, my_a, outer), nearest(step % inner, my_b, inner)

    @pl.loop(0, steps + 1)
    def _(step):
        @pl.when((step > 0) & (step < steps))
        def _():
            a, b = place_at(step)
            chunk_copy(index(a, b, core), 4, sibling).wait_recv()
            forwards(a, b, lambda copy: copy.start())

        before = place_at(jnp.maximum(step - 1, 0))
        now = place_at(jnp.minimum(step, steps - 1))
        other, source = index(*before, 1 - core), index(*now, core)

        @pl.when(step > 0)
        def _():
            chunk_copy(other, 4, sibling).wait_recv()
            products(other, 0)

        @pl.when(step < steps)
        def _():
            products(source, 1)

        has_other = jnp.where(step > 0, 1, 0)
        has_own = jnp.where(step < steps, 1, 0)

        @pl.loop(0, n_cand // 4)
        def _(group):
            for at in range(4):
                c = group * 4 + at
                first = chosen(other, cands[1, c], has_other)
                second = chosen(source, cands[1, c], has_own)
                acc[c] = acc[c] + (sums[0, first] + sums[1, second])

        @pl.when(step < steps)
        def _():
            for at in range(turned):
                c = step * turned + at
                xt[c] = tok[cands[0, c]].T

    wait_columns(og, load_sem.at[2])
    position = me * blk + lax.broadcasted_iota(jnp.int32, (blk, 1), 0)
    usable = jnp.where(position < counts[0], 1.0, 0.0)

    def term(c):
        slope = gelu_slope(acc[c])
        pre_grad = og[cands[1, c]].astype(jnp.float32) * slope * usable
        return jnp.dot(xt[c], pre_grad.astype(jnp.bfloat16), preferred_element_type=jnp.float32)

    def a_copy(a, b):
        at = a * inner + b
        return pltpu.make_async_remote_copy(
            src_ref=send_a.at[at], dst_ref=recv_a.at[at],
            send_sem=a_send.at[at], recv_sem=a_recv.at[at],
            device_id={"fsdp": sibling}, device_id_type=MESH,
        )

    def c_copy(a, b):
        return pltpu.make_async_remote_copy(
            src_ref=send_c.at[b, a], dst_ref=recv_c.at[dp, my_b, a],
            send_sem=c_send.at[b, a], recv_sem=c_recv.at[dp, my_b, a],
            device_id={"dp": a % n_dp, "fsdp": index(my_a, b, core)}, device_id_type=MESH,
        )

    def c_arrival(group, b, a):
        return pltpu.make_async_remote_copy(
            src_ref=recv_c.at[group, b, a], dst_ref=recv_c.at[group, b, a],
            send_sem=c_send.at[b, a], recv_sem=c_recv.at[group, b, a],
            device_id={"fsdp": sibling}, device_id_type=MESH,
        )

    def d_copy(a, group):
        return pltpu.make_async_remote_copy(
            src_ref=send_d.at[a], dst_ref=recv_d.at[my_a],
            send_sem=d_send.at[a, group], recv_sem=d_recv.at[my_a],
            device_id={"dp": group, "fsdp": index(a, my_b, core)}, device_id_type=MESH,
        )

    def d_arrival(a):
        return pltpu.make_async_remote_copy(
            src_ref=recv_d.at[a], dst_ref=recv_d.at[a],
            send_sem=d_send.at[0, 0], recv_sem=d_recv.at[a],
            device_id={"fsdp": sibling}, device_id_type=MESH,
        )

    def every(act):
        @pl.loop(1, inner + 1)
        def _(step):
            b = (my_b + step) % inner

            @pl.loop(0, outer // 2)
            def _(pair):
                act(b, [(dp + 1 + pair) % 2 + 2 * at for at in range(2)])

    def for_sibling(b, pair):
        found = [term(index(a, b, 1 - core)) for a in pair]
        for a, value in zip(pair, found):
            send_a[a * inner + b] = value.astype(jnp.bfloat16)
            a_copy(a, b).start()

    every(for_sibling)

    def for_mine(b, pair):
        found = [term(index(a, b, core)) for a in pair]
        for at, value in enumerate(found):
            own_a[at] = value
        for at, a in enumerate(pair):
            a_copy(a, b).wait_recv()
            total = own_a[at] + recv_a[a * inner + b].astype(jnp.float32)

            here = (b == my_b) & (a % n_dp == dp)

            @pl.when(jnp.logical_not(here))
            def _():
                send_c[b, a] = total.astype(jnp.bfloat16)
                c_copy(a, b).start()

            @pl.when(here)
            def _():
                own_c[a] = total

    every(for_mine)

    @pl.loop(1, outer + 1)
    def _(hop):
        a = (my_a + hop) % outer

        @pl.when(a % n_dp == dp)
        def _():
            @pl.loop(1, n_dp * inner)
            def _(step):
                group = (dp + step // inner) % n_dp
                b = (my_b + step % inner) % inner
                c_arrival(group, b, a).wait_recv()
                own_c[a] = own_c[a] + recv_c[group, b, a].astype(jnp.float32)

            send_d[a] = own_c[a].astype(jnp.bfloat16)

            @pl.loop(1, n_dp + 1)
            def _(step):
                group = (dp + step) % n_dp

                @pl.when((group != dp) | (a != my_a))
                def _():
                    d_copy(a, group).start()

            @pl.when(a == my_a)
            def _():
                recv_d[my_a] = send_d[a]

    own_a[0] = jnp.zeros((blk, blk), jnp.float32)

    @pl.loop(0, outer)
    def _(a):
        @pl.when((a != my_a) | (my_a % n_dp != dp))
        def _():
            d_arrival(a).wait_recv()

        own_a[0] = own_a[0] + recv_d[a].astype(jnp.float32)

    total = own_a[0]
    scale = (blk * n_dp * n_f) ** (-0.5)
    total = total * scale
    grad_out[0] = total
    score = jnp.sqrt(jnp.sum(total * total, keepdims=True) * (1.0 / (blk * blk)) + 1e-06)
    score_out[0] = score[0, 0]

    @pl.loop(1, n_f)
    def _(step):
        meta_copy(step).wait_send()

    @pl.loop(0, outer)
    def _(a):
        @pl.loop(0, inner)
        def _(b):
            forwards(a, b, lambda copy: copy.wait_send())
            a_copy(a, b).wait_send()

            @pl.when((b != my_b) | (a % n_dp != dp))
            def _():
                c_copy(a, b).wait_send()

        @pl.when(a % n_dp == dp)
        def _():
            @pl.loop(0, n_dp)
            def _(group):
                @pl.when((group != dp) | (a != my_a))
                def _():
                    d_copy(a, group).wait_send()


def per_device(
    n_dp, n_f,
    tokens, out_grad, block_values, active_blocks, drop_slots, cand_blocks, group_counts
):
    rows, _ = tokens.shape
    stored, blk, _ = block_values.shape
    n_cand = cand_blocks.shape[0]
    outer = 4
    inner = n_f // (2 * outer)
    kept = stored - 1
    bf16, f32, i32 = jnp.bfloat16, jnp.float32, jnp.int32
    half = n_cand // 2
    sem = pltpu.SemaphoreType.DMA
    return pl.pallas_call(
        functools.partial(kernel, (n_dp, n_f, outer, inner)),
        out_shape=(
            jax.ShapeDtypeStruct((1, blk, blk), f32),
            jax.ShapeDtypeStruct((1,), f32),
        ),
        in_specs=[pl.BlockSpec(memory_space=pl.ANY)] * 3
        + [pl.BlockSpec(memory_space=pltpu.SMEM)] * 4,
        out_specs=(
            pl.BlockSpec(memory_space=pltpu.VMEM),
            pl.BlockSpec(memory_space=pltpu.SMEM),
        ),
        scratch_shapes=[
            pltpu.VMEM((tokens.shape[1] // blk, rows, blk), bf16),
            pltpu.VMEM((out_grad.shape[1] // blk, rows, blk), bf16),
            pltpu.VMEM(block_values.shape, bf16),
            pltpu.VMEM((n_f, kept * blk, blk), bf16),
            pltpu.VMEM((n_f, 1, 128), i32),
            pltpu.SMEM((n_f, 1, 128), i32),
            pltpu.VMEM((n_cand, blk, rows), bf16),
            pltpu.VMEM((2, 1 << kept, rows, blk), f32),
            pltpu.VMEM((n_cand, rows, blk), f32),
            pltpu.VMEM((half, blk, blk), bf16),
            pltpu.VMEM((half, blk, blk), bf16),
            pltpu.VMEM((2, blk, blk), f32),
            pltpu.VMEM((inner, outer, blk, blk), bf16),
            pltpu.VMEM((n_dp, inner, outer, blk, blk), bf16),
            pltpu.VMEM((outer, blk, blk), f32),
            pltpu.VMEM((outer, blk, blk), bf16),
            pltpu.VMEM((outer, blk, blk), bf16),
            sem((3,)), sem((n_f,)), sem((n_f,)), sem(()), sem((5, n_f)), sem((n_f,)),
            sem((half,)), sem((half,)), sem((inner, outer)), sem((n_dp, inner, outer)),
            sem((outer, n_dp)), sem((outer,)),
        ],
        compiler_params=pltpu.CompilerParams(
            collective_id=0, has_side_effects=True, vmem_limit_bytes=64 * 1024 * 1024 - 128 * 1024
        ),
        cost_estimate=pl.CostEstimate(
            flops=2 * blk ** 3 * (n_f * kept + n_cand),
            bytes_accessed=2 * (tokens.size + out_grad.size),
            transcendentals=n_cand * blk * blk,
        ),
    )(
        tokens, out_grad, block_values, active_blocks.T, drop_slots, cand_blocks.T, group_counts
    )


def solution(mesh):
    return jax.shard_map(
        functools.partial(per_device, mesh.shape["dp"], mesh.shape["fsdp"]),
        mesh=mesh,
        in_specs=(
            P(("dp", "fsdp"), None),
            P(("dp", "fsdp"), None),
            P("fsdp", None, None),
            P("fsdp", None),
            P("fsdp"),
            P(),
            P("dp"),
        ),
        out_specs=(P("fsdp", None, None), P("fsdp")),
        check_vma=False,
    )
```

```python
import functools
import jax
import jax.numpy as jnp
from jax import lax
from jax.experimental import pallas as pl
from jax.experimental.pallas import tpu as pltpu
from jax.sharding import PartitionSpec as P

MESH = pl.DeviceIdType.MESH


def gelu_slope(value_in):
    normal_cdf = 0.5 * (1.0 + lax.erf(value_in * 0.7071067811865476))
    density = jnp.exp(-0.5 * value_in * value_in) * 0.3989422804014327
    return normal_cdf + value_in * density


def kernel(
    dims,
    tok_hbm, og_hbm, bv_hbm, active, drops, cands, counts,
    grad_out, score_out,
    tok, og, bv, gath, meta_v, meta_s, xt, sums, acc,
    send_a, recv_a, own_a, send_c, recv_c, own_c, send_d, recv_d,
    load_sem, meta_send, meta_recv, meta_load, chunk_send, chunk_recv,
    a_send, a_recv, c_send, c_recv, d_send, d_recv,
):
    n_dp, n_f, outer, inner = dims
    blk = bv.shape[1]
    stored = bv.shape[0]
    kept = stored - 1
    split = kept // 2
    n_cand = acc.shape[0]
    dp = lax.axis_index("dp")
    me = lax.axis_index("fsdp")
    core = me % 2
    my_b = (me // 2) % inner
    my_a = me // (2 * inner)
    sibling = me + 1 - 2 * core

    def index(a, b, c):
        return (a * inner + b) * 2 + c

    load_bv = pltpu.make_async_copy(bv_hbm, bv, load_sem.at[0])
    load_bv.start()

    def load_columns(hbm, held, sem):
        @pl.loop(0, held.shape[0])
        def _(at):
            column = pl.multiple_of(at * blk, blk)
            pltpu.make_async_copy(hbm.at[:, pl.ds(column, blk)], held.at[at], sem).start()

    def wait_columns(held, sem):
        pltpu.make_async_copy(held, held, sem).wait()

    barrier = pltpu.get_barrier_semaphore()

    @pl.loop(1, n_f)
    def _(step):
        pl.semaphore_signal(
            barrier, inc=1, device_id={"fsdp": (me + step) % n_f}, device_id_type=MESH
        )

    @pl.loop(1, n_dp)
    def _(step):
        def greet(a, b):
            pl.semaphore_signal(
                barrier,
                inc=1,
                device_id={"dp": (dp + step) % n_dp, "fsdp": index(a, b, core)},
                device_id_type=MESH,
            )

        @pl.loop(0, inner)
        def _(b):
            greet(my_a, b)

        @pl.loop(1, outer)
        def _(hop):
            greet((my_a + hop) % outer, my_b)

    load_columns(tok_hbm, tok, load_sem.at[1])
    drop = drops[0]
    lane = lax.broadcasted_iota(jnp.int32, (1, 128), 1)
    places = jnp.zeros((1, 128), jnp.int32)
    load_bv.wait()
    for slot in range(kept):
        at = slot + jnp.where(drop <= slot, 1, 0)
        gath[me, slot // split, slot % split * blk:(slot % split + 1) * blk, :] = bv[at]
        places = jnp.where(lane == 2 * slot, active[0, at], places)
        places = jnp.where(lane == 2 * slot + 1, active[1, at], places)
    meta_v[me] = places

    pl.semaphore_wait(barrier, n_f - 1 + (n_dp - 1) * (inner + outer - 1))

    def chunk_copy(source, half, way, target):
        return pltpu.make_async_remote_copy(
            src_ref=gath.at[source, half],
            dst_ref=gath.at[source, half],
            send_sem=chunk_send.at[way, source, half],
            recv_sem=chunk_recv.at[source, half],
            device_id={"fsdp": target},
            device_id_type=MESH,
        )

    def meta_copy(step):
        target = (me + step) % n_f
        return pltpu.make_async_remote_copy(
            src_ref=meta_v.at[me],
            dst_ref=meta_v.at[me],
            send_sem=meta_send.at[step],
            recv_sem=meta_recv.at[me],
            device_id={"fsdp": target},
            device_id_type=MESH,
        )

    def meta_arrival(source):
        return pltpu.make_async_remote_copy(
            src_ref=meta_v.at[source],
            dst_ref=meta_v.at[source],
            send_sem=meta_send.at[0],
            recv_sem=meta_recv.at[source],
            device_id={"fsdp": sibling},
            device_id_type=MESH,
        )

    def forwards(a, b, half, act):
        source = index(a, b, core)

        @pl.when((b == my_b) & (a >= my_a) & (my_a > 0))
        def _():
            act(chunk_copy(source, half, 0, index(my_a - 1, my_b, core)))

        @pl.when((b == my_b) & (a <= my_a) & (my_a < outer - 1))
        def _():
            act(chunk_copy(source, half, 1, index(my_a + 1, my_b, core)))

        @pl.when((b >= my_b) & (my_b > 0))
        def _():
            act(chunk_copy(source, half, 2, index(my_a, my_b - 1, core)))

        @pl.when((b <= my_b) & (my_b < inner - 1))
        def _():
            act(chunk_copy(source, half, 3, index(my_a, my_b + 1, core)))

        act(chunk_copy(source, half, 4, sibling))

    def around(step, mine):
        return mine + (1 - 2 * (step % 2)) * ((step + 1) // 2)

    @pl.loop(1, n_f)
    def _(step):
        meta_copy(step).start()

    for half in range(2):
        forwards(my_a, my_b, half, lambda copy: copy.start())
    load_columns(og_hbm, og, load_sem.at[2])
    wait_columns(tok, load_sem.at[1])
    acc[...] = jnp.zeros(acc.shape, jnp.float32)

    @pl.loop(1, n_f)
    def _(step):
        meta_arrival((me + step) % n_f).wait_recv()

    to_scalars = pltpu.make_async_copy(meta_v, meta_s, meta_load)
    to_scalars.start()
    to_scalars.wait()

    for turn in range(2):
        sums[turn, 0] = jnp.zeros(sums.shape[2:], jnp.float32)

    def products(source, turn):
        for slot in range(kept):
            sums[turn, 1 << slot] = jnp.dot(
                tok[meta_s[source, 0, 2 * slot]],
                gath[source, slot // split, slot % split * blk:(slot % split + 1) * blk, :],
                preferred_element_type=jnp.float32,
            )

        @pl.loop(0, blk // 32)
        def _(part):
            rows = pl.ds(pl.multiple_of(part * 32, 32), 32)
            found = [None] * (1 << kept)
            for slot in range(kept):
                found[1 << slot] = sums[turn, 1 << slot, rows, :]
                for low in range(1, 1 << slot):
                    found[low + (1 << slot)] = found[low] + found[1 << slot]
                    sums[turn, low + (1 << slot), rows, :] = found[low + (1 << slot)]

    def chosen(source, column, valid):
        bits = jnp.int32(0)
        for slot in range(kept):
            bits = bits + jnp.where(meta_s[source, 0, 2 * slot + 1] == column, 1 << slot, 0)
        return bits * valid

    turned = n_cand // (outer * inner)

    steps = outer * inner

    def nearest(step, mine, size):
        ends = jnp.minimum(mine, size - 1 - mine)
        rest = jnp.where(mine < size - 1 - mine, step, size - 1 - step)
        return jnp.where(step <= 2 * ends, around(step, mine), rest)

    def place_at(step):
        return nearest(step // inner, my_a, outer), nearest(step % inner, my_b, inner)

    @pl.loop(0, steps + 1)
    def _(step):
        @pl.when((step > 0) & (step < steps))
        def _():
            a, b = place_at(step)

            @pl.loop(0, 2)
            def _(half):
                chunk_copy(index(a, b, core), half, 4, sibling).wait_recv()
                forwards(a, b, half, lambda copy: copy.start())

        before = place_at(jnp.maximum(step - 1, 0))
        now = place_at(jnp.minimum(step, steps - 1))
        other, source = index(*before, 1 - core), index(*now, core)

        @pl.when(step > 0)
        def _():
            for half in range(2):
                chunk_copy(other, half, 4, sibling).wait_recv()
            products(other, 0)

        @pl.when(step < steps)
        def _():
            products(source, 1)

        has_other = jnp.where(step > 0, 1, 0)
        has_own = jnp.where(step < steps, 1, 0)

        @pl.loop(0, n_cand // 4)
        def _(group):
            for at in range(4):
                c = group * 4 + at
                first = chosen(other, cands[1, c], has_other)
                second = chosen(source, cands[1, c], has_own)
                acc[c] = acc[c] + (sums[0, first] + sums[1, second])

        @pl.when(step < steps)
        def _():
            for at in range(turned):
                c = step * turned + at
                xt[c] = tok[cands[0, c]].T

    wait_columns(og, load_sem.at[2])
    position = me * blk + lax.broadcasted_iota(jnp.int32, (blk, 1), 0)
    usable = jnp.where(position < counts[0], 1.0, 0.0)

    def term(c):
        slope = gelu_slope(acc[c])
        pre_grad = og[cands[1, c]].astype(jnp.float32) * slope * usable
        return jnp.dot(xt[c], pre_grad.astype(jnp.bfloat16), preferred_element_type=jnp.float32)

    def a_copy(a, b):
        at = a * inner + b
        return pltpu.make_async_remote_copy(
            src_ref=send_a.at[at], dst_ref=recv_a.at[at],
            send_sem=a_send.at[at], recv_sem=a_recv.at[at],
            device_id={"fsdp": sibling}, device_id_type=MESH,
        )

    def c_copy(a, b):
        return pltpu.make_async_remote_copy(
            src_ref=send_c.at[b, a], dst_ref=recv_c.at[dp, my_b, a],
            send_sem=c_send.at[b, a], recv_sem=c_recv.at[dp, my_b, a],
            device_id={"dp": a % n_dp, "fsdp": index(my_a, b, core)}, device_id_type=MESH,
        )

    def c_arrival(group, b, a):
        return pltpu.make_async_remote_copy(
            src_ref=recv_c.at[group, b, a], dst_ref=recv_c.at[group, b, a],
            send_sem=c_send.at[b, a], recv_sem=c_recv.at[group, b, a],
            device_id={"fsdp": sibling}, device_id_type=MESH,
        )

    def d_copy(a, group):
        return pltpu.make_async_remote_copy(
            src_ref=send_d.at[a], dst_ref=recv_d.at[my_a],
            send_sem=d_send.at[a, group], recv_sem=d_recv.at[my_a],
            device_id={"dp": group, "fsdp": index(a, my_b, core)}, device_id_type=MESH,
        )

    def d_arrival(a):
        return pltpu.make_async_remote_copy(
            src_ref=recv_d.at[a], dst_ref=recv_d.at[a],
            send_sem=d_send.at[0, 0], recv_sem=d_recv.at[a],
            device_id={"fsdp": sibling}, device_id_type=MESH,
        )

    def every(act):
        @pl.loop(1, inner + 1)
        def _(step):
            b = (my_b + step) % inner

            @pl.loop(0, outer // 2)
            def _(pair):
                act(b, [(dp + 1 + pair) % 2 + 2 * at for at in range(2)])

    def for_sibling(b, pair):
        found = [term(index(a, b, 1 - core)) for a in pair]
        for a, value in zip(pair, found):
            send_a[a * inner + b] = value.astype(jnp.bfloat16)
            a_copy(a, b).start()

    every(for_sibling)

    def for_mine(b, pair):
        found = [term(index(a, b, core)) for a in pair]
        for at, value in enumerate(found):
            own_a[at] = value
        for at, a in enumerate(pair):
            a_copy(a, b).wait_recv()
            total = own_a[at] + recv_a[a * inner + b].astype(jnp.float32)

            here = (b == my_b) & (a % n_dp == dp)

            @pl.when(jnp.logical_not(here))
            def _():
                send_c[b, a] = total.astype(jnp.bfloat16)
                c_copy(a, b).start()

            @pl.when(here)
            def _():
                own_c[a] = total

    every(for_mine)

    @pl.loop(1, n_f)
    def _(step):
        meta_copy(step).wait_send()

    @pl.loop(0, steps)
    def _(step):
        a, b = step // inner, step % inner
        for half in range(2):
            forwards(a, b, half, lambda copy: copy.wait_send())

    @pl.loop(1, outer + 1)
    def _(hop):
        a = (my_a + hop) % outer

        @pl.when(a % n_dp == dp)
        def _():
            @pl.loop(1, n_dp * inner)
            def _(step):
                group = (dp + step // inner) % n_dp
                b = (my_b + step % inner) % inner
                c_arrival(group, b, a).wait_recv()
                own_c[a] = own_c[a] + recv_c[group, b, a].astype(jnp.float32)

            send_d[a] = own_c[a].astype(jnp.bfloat16)

            @pl.loop(1, n_dp + 1)
            def _(step):
                group = (dp + step) % n_dp

                @pl.when((group != dp) | (a != my_a))
                def _():
                    d_copy(a, group).start()

            @pl.when(a == my_a)
            def _():
                recv_d[my_a] = send_d[a]

    @pl.loop(0, steps)
    def _(step):
        a, b = step // inner, step % inner
        a_copy(a, b).wait_send()

        @pl.when((b != my_b) | (a % n_dp != dp))
        def _():
            c_copy(a, b).wait_send()

    own_a[0] = jnp.zeros((blk, blk), jnp.float32)

    @pl.loop(0, outer)
    def _(a):
        @pl.when((a != my_a) | (my_a % n_dp != dp))
        def _():
            d_arrival(a).wait_recv()

        own_a[0] = own_a[0] + recv_d[a].astype(jnp.float32)

    total = own_a[0]
    scale = (blk * n_dp * n_f) ** (-0.5)
    total = total * scale
    grad_out[0] = total
    score = jnp.sqrt(jnp.sum(total * total, keepdims=True) * (1.0 / (blk * blk)) + 1e-06)
    score_out[0] = score[0, 0]

    @pl.loop(0, outer)
    def _(a):
        @pl.when(a % n_dp == dp)
        def _():
            @pl.loop(0, n_dp)
            def _(group):
                @pl.when((group != dp) | (a != my_a))
                def _():
                    d_copy(a, group).wait_send()


def per_device(
    n_dp, n_f,
    tokens, out_grad, block_values, active_blocks, drop_slots, cand_blocks, group_counts
):
    rows, _ = tokens.shape
    stored, blk, _ = block_values.shape
    n_cand = cand_blocks.shape[0]
    outer = 4
    inner = n_f // (2 * outer)
    kept = stored - 1
    bf16, f32, i32 = jnp.bfloat16, jnp.float32, jnp.int32
    half = n_cand // 2
    sem = pltpu.SemaphoreType.DMA
    return pl.pallas_call(
        functools.partial(kernel, (n_dp, n_f, outer, inner)),
        out_shape=(
            jax.ShapeDtypeStruct((1, blk, blk), f32),
            jax.ShapeDtypeStruct((1,), f32),
        ),
        in_specs=[pl.BlockSpec(memory_space=pl.ANY)] * 3
        + [pl.BlockSpec(memory_space=pltpu.SMEM)] * 4,
        out_specs=(
            pl.BlockSpec(memory_space=pltpu.VMEM),
            pl.BlockSpec(memory_space=pltpu.SMEM),
        ),
        scratch_shapes=[
            pltpu.VMEM((tokens.shape[1] // blk, rows, blk), bf16),
            pltpu.VMEM((out_grad.shape[1] // blk, rows, blk), bf16),
            pltpu.VMEM(block_values.shape, bf16),
            pltpu.VMEM((n_f, 2, kept // 2 * blk, blk), bf16),
            pltpu.VMEM((n_f, 1, 128), i32),
            pltpu.SMEM((n_f, 1, 128), i32),
            pltpu.VMEM((n_cand, blk, rows), bf16),
            pltpu.VMEM((2, 1 << kept, rows, blk), f32),
            pltpu.VMEM((n_cand, rows, blk), f32),
            pltpu.VMEM((half, blk, blk), bf16),
            pltpu.VMEM((half, blk, blk), bf16),
            pltpu.VMEM((2, blk, blk), f32),
            pltpu.VMEM((inner, outer, blk, blk), bf16),
            pltpu.VMEM((n_dp, inner, outer, blk, blk), bf16),
            pltpu.VMEM((outer, blk, blk), f32),
            pltpu.VMEM((outer, blk, blk), bf16),
            pltpu.VMEM((outer, blk, blk), bf16),
            sem((3,)), sem((n_f,)), sem((n_f,)), sem(()), sem((5, n_f, 2)), sem((n_f, 2)),
            sem((half,)), sem((half,)), sem((inner, outer)), sem((n_dp, inner, outer)),
            sem((outer, n_dp)), sem((outer,)),
        ],
        compiler_params=pltpu.CompilerParams(
            collective_id=0, has_side_effects=True, vmem_limit_bytes=64 * 1024 * 1024 - 128 * 1024
        ),
        cost_estimate=pl.CostEstimate(
            flops=2 * blk ** 3 * (n_f * kept + n_cand),
            bytes_accessed=2 * (tokens.size + out_grad.size),
            transcendentals=n_cand * blk * blk,
        ),
    )(
        tokens, out_grad, block_values, active_blocks.T, drop_slots, cand_blocks.T, group_counts
    )


def solution(mesh):
    return jax.shard_map(
        functools.partial(per_device, mesh.shape["dp"], mesh.shape["fsdp"]),
        mesh=mesh,
        in_specs=(
            P(("dp", "fsdp"), None),
            P(("dp", "fsdp"), None),
            P("fsdp", None, None),
            P("fsdp", None),
            P("fsdp"),
            P(),
            P("dp"),
        ),
        out_specs=(P("fsdp", None, None), P("fsdp")),
        check_vma=False,
    )
```
